32 devices in a mesh: groups: 2 (over y), blk: 4 (over z), slab: 2 (over x), ch: 2 (over core).
Axes of the slice: x: 2, y: 2, z: 4, core: 2. Of those that a mesh axis runs over, the one named last changes fastest.
Arguments:
- fine_input: bfloat16 [8, 4, 4, 256, 128], P(('groups', 'slab', 'ch'), 'blk'), parts along dimension 0, may hold values from -6 to 6
- cotangent: bfloat16 [8, 4, 4, 256, 128], P(('groups', 'slab', 'ch'), 'blk'), parts along dimension 0, may hold values from -6 to 6
- conv_weight: bfloat16 [27, 128, 128], replicated, may hold values from -0.109375 to 0.109375
- down_weight: bfloat16 [128, 256], replicated, may hold values from -0.5 to 0.5
- depth_weight: bfloat16 [27, 256], replicated, may hold values from -1.25 to 1.25
- up_weight: bfloat16 [256, 128], replicated, may hold values from -0.375 to 0.375
- slot_x: int32 [8, 4, 4], P(('groups', 'slab', 'ch'), 'blk'), parts along dimension 0, may hold values from -1 to 11, as said below
- neighbours: int32 [8, 4, 4, 27], P(('groups', 'slab', 'ch'), 'blk'), parts along dimension 0, may hold values from -1 to 3, as said below
Outputs:
- input_grad: bfloat16 [8, 4, 4, 256, 128], P(('groups', 'slab', 'ch'), 'blk'), parts along dimension 0
- conv_grad: float32 [54, 16384], P('groups', ('blk', 'slab', 'ch')), parts along dimension 0
- down_grad: float32 [256, 256], P('groups'), parts along dimension 0
- depth_grad: float32 [54, 256], P('groups'), parts along dimension 0
- up_grad: float32 [512, 128], P('groups'), parts along dimension 0
The draws below stay inside these ranges and needn't reach their ends.
There are 2 independent parts, one for each index of `groups`. The reference program is written for one: setup_inputs(seed, part) draws one part's arguments, and reference() takes and returns one part's arrays. A program takes and returns all parts, laid end to end along the dimension named above; an argument that names none is the same for every part. Nothing has to cross between parts.
Inputs may be any that keep to these rules, and one draw needn't show every extreme that they name: `slot_x`: each device row of 4 entries lists distinct x block indices, occupied slots first and -1 in the rest. Rows 2m and 2m + 1 of the first dimension hold the two z halves of the same blocks in the same slots. Some row holds 4 blocks. `neighbours`: entry 9a + 3b + e of slot k at row j, column i gives the slot, in row j + a - 1 and column i + b - 1, of the occupied block at x block index slot_x[j, i, k] + e - 1, or -1 where that block is unoccupied or outside the grid; every entry of an empty slot is -1.
All inputs are finite; a program needn't handle non-finite values.
Results may differ from the reference program's by a relative error of at most 0.0068.
Values may be sent and summed in bfloat16 or wider, within the bound.
A program may use at most 64 MiB of HBM per device.

```python
import jax
import jax.numpy as jnp
from jax import lax

C = 128
CC = 256
GX = 12
SLOTS = 4
HV = 256
ZD = 4
YB = 4
N_SLAB = 2


def occupancy(key):
    key_count, key_place = jax.random.split(key)
    levels = jnp.array([0, 0, 1, 1, 1, 2, 2, SLOTS], jnp.int32)
    picked = jax.random.randint(key_count, (N_SLAB, YB), 0, 8)
    counts = levels[picked]
    counts = counts.at[0, 0].set(SLOTS)
    scores = jax.random.randint(key_place, (N_SLAB, YB, GX), 0, 1 << 20) * GX + jnp.arange(GX, dtype=jnp.int32)
    ordered = jnp.argsort(scores, axis=-1).astype(jnp.int32)[..., :SLOTS]
    living = jnp.arange(SLOTS, dtype=jnp.int32)[None, None, :] < counts[..., None]
    return jnp.where(living, ordered, -1)


def draw_slot_x(key, part):
    blocks = occupancy(key)
    return jnp.repeat(blocks, ZD // N_SLAB, axis=0).astype(jnp.int32)


def draw_neighbours(key, part):
    blocks = jnp.repeat(occupancy(key), ZD // N_SLAB, axis=0)
    positions = jnp.arange(GX, dtype=jnp.int32)
    slot_ids = jnp.arange(SLOTS, dtype=jnp.int32)
    matches = blocks[..., None] == positions[None, None, None, :]
    owner_grid = jnp.max(jnp.where(matches, slot_ids[None, None, :, None], -1), axis=2)
    padded = jnp.pad(owner_grid, ((1, 1), (1, 1), (1, 1)), constant_values=-1)
    entries = []
    for depth_at in range(3):
        for row_at in range(3):
            for col_at in range(3):
                window = padded[depth_at:depth_at + ZD, row_at:row_at + YB, :]
                looked = jnp.take_along_axis(window, jnp.maximum(blocks, 0) + col_at, axis=2)
                entries.append(jnp.where(blocks >= 0, looked, -1))
    return jnp.stack(entries, axis=-1).astype(jnp.int32)


def shard_levels(key, shape, cuts, smallest, largest):
    gain = 1.0
    for position, parts in cuts:
        draws = jax.random.uniform(jax.random.fold_in(jax.random.fold_in(key, 6), position), (parts,), jnp.float32, smallest / len(cuts), largest / len(cuts))
        gain = gain * jnp.repeat(jnp.exp(draws), shape[position] // parts).reshape((-1,) + (1,) * (len(shape) - 1 - position))
    return gain


def bell_draw(own_key, shape, scale, limit, cuts=(), kind=jnp.bfloat16):
    values = jax.random.normal(own_key, shape, jnp.float32) * scale
    if len(cuts) > 0:
        values = shard_levels(own_key, shape, cuts, -0.22, 0.18) * values
    return jnp.clip(values, min=-limit, max=limit).astype(kind)


def setup_inputs(seed: int = 0, part: int = 0) -> dict:
    arg_keys = jax.random.split(jax.random.key(seed), 9)
    own_keys = jax.random.split(jax.random.fold_in(arg_keys[8], part), 9)
    return {
        "fine_input": bell_draw(own_keys[0], (ZD, YB, SLOTS, HV, C), 1.0, 6.0, ((0, 4), (1, 4))),
        "cotangent": bell_draw(own_keys[1], (ZD, YB, SLOTS, HV, C), 1.0, 6.0, ((0, 4), (1, 4))),
        "conv_weight": bell_draw(arg_keys[2], (27, C, C), (27 * C) ** -0.5, 0.109375),
        "down_weight": bell_draw(arg_keys[3], (C, CC), C ** -0.5, 0.5),
        "depth_weight": bell_draw(arg_keys[4], (27, CC), 27 ** -0.5, 1.25),
        "up_weight": bell_draw(arg_keys[5], (CC, C), CC ** -0.5, 0.375),
        "slot_x": draw_slot_x(jax.random.fold_in(jax.random.fold_in(arg_keys[8], part), 71), part),
        "neighbours": draw_neighbours(jax.random.fold_in(jax.random.fold_in(arg_keys[8], part), 71), part),
    }


def silu_slope(value):
    sigma = jax.nn.sigmoid(value)
    return sigma * (1.0 + value * (1.0 - sigma))


def shifted_rows(tile, flip):
    blocks = []
    for depth_at in range(3):
        for row_at in range(3):
            for col_at in range(3):
                if flip:
                    start_z, start_y, start_x = 2 - depth_at, 2 - row_at, 2 - col_at
                else:
                    start_z, start_y, start_x = depth_at, row_at, col_at
                blocks.append(tile[start_z:start_z + 4, start_y:start_y + 8, start_x:start_x + 8].reshape(256, tile.shape[-1]))
    return jnp.concatenate(blocks, axis=1)


def assemble(padded, row, col, linked_row):
    bounds_z = ((3, 4), (0, 4), (0, 1))
    bounds_w = ((7, 8), (0, 8), (0, 1))
    anchor = jnp.zeros((), jnp.int32)
    layers = []
    for depth_at in range(3):
        strips = []
        for row_at in range(3):
            pieces = []
            for col_at in range(3):
                linked = linked_row[9 * depth_at + 3 * row_at + col_at].astype(jnp.int32)
                starts = ((row + depth_at).astype(jnp.int32), (col + row_at).astype(jnp.int32), jnp.maximum(linked, anchor).astype(jnp.int32), anchor, anchor, anchor, anchor)
                whole = lax.dynamic_slice(padded, starts, (1, 1, 1, 4, 8, 8, padded.shape[-1]))[0, 0, 0]
                portion = whole[bounds_z[depth_at][0]:bounds_z[depth_at][1], bounds_w[row_at][0]:bounds_w[row_at][1], bounds_w[col_at][0]:bounds_w[col_at][1]]
                pieces.append(jnp.where(linked >= 0, portion, jnp.zeros_like(portion)))
            strips.append(jnp.concatenate(pieces, axis=2))
        layers.append(jnp.concatenate(strips, axis=1))
    return jnp.concatenate(layers, axis=0)


def spread(framed, depth, flip, size_z, size_y, size_x):
    total = jnp.zeros((size_z, size_y, size_x, depth.shape[1]), jnp.float32)
    for index in range(27):
        start_z, start_y, start_x = index // 9, index // 3 % 3, index % 3
        if flip:
            start_z, start_y, start_x = 2 - start_z, 2 - start_y, 2 - start_x
        total = total + framed[start_z:start_z + size_z, start_y:start_y + size_y, start_x:start_x + size_x].astype(jnp.float32) * depth[index]
    return total


def reference(fine_input, cotangent, conv_weight, down_weight, depth_weight, up_weight, slot_x, neighbours):
    total = ZD * YB * SLOTS
    pad_spec = ((1, 1), (1, 1), (0, 0), (0, 0), (0, 0), (0, 0), (0, 0))
    padded_in = jnp.pad(fine_input.reshape(ZD, YB, SLOTS, 4, 8, 8, C), pad_spec)
    alive = (slot_x >= 0).reshape(total)
    flat_index = jnp.arange(total, dtype=jnp.int32)
    rows_of = (flat_index // (YB * SLOTS)).astype(jnp.int32)
    cols_of = (flat_index // SLOTS % YB).astype(jnp.int32)
    links = neighbours.reshape(total, 27).astype(jnp.int32)
    kernel = conv_weight.astype(jnp.float32).reshape(27 * C, C)
    back_kernel = jnp.transpose(conv_weight.astype(jnp.float32), (0, 2, 1)).reshape(27 * C, C)
    hi = lax.Precision.HIGHEST

    def forward_one(inputs):
        row, col, linked_row, living = inputs

        def work(_):
            tile = assemble(padded_in, row, col, linked_row).astype(jnp.float32)
            return jnp.dot(shifted_rows(tile, False), kernel, precision=hi)

        return lax.cond(living, work, lambda _: jnp.zeros((256, C), jnp.float32), None)

    field = lax.map(forward_one, (rows_of, cols_of, links, alive))
    livef = alive.astype(jnp.float32)[:, None, None]
    active = jax.nn.silu(field) * livef
    pooled = active.reshape(ZD, YB, SLOTS, 4, 2, 4, 2, 4, C).mean(axis=(3, 5, 7))
    select = (slot_x[..., None] == jnp.arange(GX, dtype=jnp.int32)).astype(jnp.float32)
    coarse_in = jnp.einsum("jbkg,jbkyxc->jbygxc", select, pooled).reshape(ZD, 2 * YB, 2 * GX, C).astype(jnp.bfloat16)
    cells = ZD * 2 * YB * 2 * GX
    coarse_rows = coarse_in.reshape(cells, C)
    grid_g = jnp.dot(coarse_rows, down_weight, preferred_element_type=jnp.float32).astype(jnp.bfloat16).reshape(ZD, 2 * YB, 2 * GX, CC)
    depth = depth_weight.astype(jnp.float32)
    framed_g = jnp.pad(grid_g, ((1, 1), (1, 1), (1, 1), (0, 0)))
    grid_v = grid_g.astype(jnp.float32) + spread(framed_g, depth, False, ZD, 2 * YB, 2 * GX)
    grid_q = jax.nn.silu(grid_v).astype(jnp.bfloat16)
    upstream = cotangent.astype(jnp.float32).reshape(total, 256, C) * livef
    cell_sums = upstream.reshape(ZD, YB, SLOTS, 4, 2, 4, 2, 4, C).sum(axis=(3, 5, 7))
    grad_z = jnp.einsum("jbkg,jbkyxc->jbygxc", select, cell_sums).reshape(cells, C).astype(jnp.bfloat16)
    up_grad = jnp.dot(grid_q.reshape(cells, CC).astype(jnp.float32).T, grad_z.astype(jnp.float32), precision=hi)
    grad_q = jnp.dot(grad_z, up_weight.T, preferred_element_type=jnp.float32)
    grad_v = (grad_q * silu_slope(grid_v.reshape(cells, CC))).astype(jnp.bfloat16).reshape(ZD, 2 * YB, 2 * GX, CC)
    framed_v = jnp.pad(grad_v, ((1, 1), (1, 1), (1, 1), (0, 0)))
    grad_g = (grad_v.astype(jnp.float32) + spread(framed_v, depth, True, ZD, 2 * YB, 2 * GX)).astype(jnp.bfloat16)
    terms = []
    for index in range(27):
        start_z, start_y, start_x = index // 9, index // 3 % 3, index % 3
        shifted = framed_g[start_z:start_z + ZD, start_y:start_y + 2 * YB, start_x:start_x + 2 * GX].astype(jnp.float32)
        terms.append(jnp.sum(shifted * grad_v.astype(jnp.float32), axis=(0, 1, 2)))
    depth_grad = jnp.stack(terms, axis=0)
    grad_rows = grad_g.reshape(cells, CC)
    down_grad = jnp.dot(coarse_rows.astype(jnp.float32).T, grad_rows.astype(jnp.float32), precision=hi)
    grad_p = jnp.dot(grad_rows, down_weight.T, preferred_element_type=jnp.float32)
    grad_p_slots = jnp.einsum("jbkg,jbygxc->jbkyxc", select, grad_p.reshape(ZD, YB, 2, GX, 2, C))
    spread_p = jnp.broadcast_to(grad_p_slots.reshape(total, 1, 2, 1, 2, 1, C), (total, 4, 2, 4, 2, 4, C)).reshape(total, 256, C)
    grad_f = ((upstream + spread_p / 64.0) * silu_slope(field) * livef).astype(jnp.bfloat16)
    padded_df = jnp.pad(grad_f.reshape(ZD, YB, SLOTS, 4, 8, 8, C), pad_spec)

    def backward_one(carry, inputs):
        row, col, linked_row, living, slot_grad = inputs

        def work(_):
            tile = assemble(padded_in, row, col, linked_row).astype(jnp.float32)
            grad_tile = assemble(padded_df, row, col, linked_row).astype(jnp.float32)
            grad_in = jnp.dot(shifted_rows(grad_tile, True), back_kernel, precision=hi)
            grad_w = jnp.dot(shifted_rows(tile, False).T, slot_grad.astype(jnp.float32), precision=hi)
            return grad_in, grad_w

        def skip(_):
            return jnp.zeros((256, C), jnp.float32), jnp.zeros((27 * C, C), jnp.float32)

        grad_in, grad_w = lax.cond(living, work, skip, None)
        return carry + grad_w, grad_in

    weight_sum, grad_inputs = lax.scan(backward_one, jnp.zeros((27 * C, C), jnp.float32), (rows_of, cols_of, links, alive, grad_f))
    input_grad = grad_inputs.astype(jnp.bfloat16).reshape(ZD, YB, SLOTS, 256, C)
    conv_grad = weight_sum.reshape(27, C * C)
    return input_grad, conv_grad, down_grad, depth_grad, up_grad
```

```python
import functools

import jax
import jax.numpy as jnp
import numpy as np
from jax import lax
from jax.experimental import pallas as pl
from jax.experimental.pallas import tpu as pltpu
from jax.sharding import PartitionSpec as P

F32 = jnp.float32
BF16 = jnp.bfloat16
HIGH = lax.Precision.HIGHEST
DIRS = [(da, db) for da in (-1, 0, 1) for db in (-1, 0, 1) if (da, db) != (0, 0)]


def silu_slope(value):
    sigma = jax.nn.sigmoid(value)
    return sigma * (1.0 + value * (1.0 - sigma))


def level_kernel(
    sizes, reduce, nb, x_in, cot_in, conv_w, down_w, depth_w, up_w, idx_in,
    dx_out, cw_out, dn_out, dp_out, up_out,
    C0, NZ, NY, NC, hz, hy, hc, sz, sy, sc, FR, T, FS, DF, WB, GA, WF,
    st1, rv1, st2, rv2, sms, smr, ag, DG,
    hs, hr, cs, cr, p1s, p1r, p2s, p2r, ss, sr, gs, gr,
):
    B, S, H = sizes
    K = 4
    blk, slab, ch = lax.axis_index("blk"), lax.axis_index("slab"), lax.axis_index("ch")
    row = slab * H + ch
    rows = S * H
    n = B * S * H
    me = blk * rows + row

    def target(d):
        return {"blk": lax.div(d, rows), "slab": lax.rem(lax.div(d, H), S), "ch": lax.rem(d, H)}

    def exists(da, db):
        r, c = row + da, blk + db
        return (r >= 0) & (r < rows) & (c >= 0) & (c < B)

    def beside(da, db):
        return target((blk + db) * rows + row + da)

    for ref in (hz, hy, hc, GA, sms):
        ref[...] = jnp.zeros(ref.shape, ref.dtype)
    C0[K] = jnp.zeros(C0.shape[1:], F32)
    NZ[:, K] = jnp.zeros((2,) + NZ.shape[2:], F32)
    NY[:, K] = jnp.zeros((2,) + NY.shape[2:], F32)
    NC[:, K] = jnp.zeros((4,) + NC.shape[2:], F32)
    barrier = pltpu.get_barrier_semaphore()
    if reduce:
        def greet(r, carry):
            pl.semaphore_signal(barrier, inc=1, device_id=target(lax.rem(me + r, n)),
                                device_id_type=pl.DeviceIdType.MESH)
            return carry
        lax.fori_loop(1, n, greet, 0)
    else:
        for da, db in DIRS:
            @pl.when(exists(da, db))
            def _():
                pl.semaphore_signal(barrier, inc=1, device_id=beside(da, db),
                                    device_id_type=pl.DeviceIdType.MESH)

    def entered():
        if reduce:
            pl.semaphore_wait(barrier, n - 1)
        else:
            for da, db in DIRS:
                @pl.when(exists(da, db))
                def _():
                    pl.semaphore_wait(barrier, 1)

    def copy(src, dst, s, r, dev):
        return pltpu.make_async_remote_copy(
            src_ref=src, dst_ref=dst, send_sem=s, recv_sem=r, device_id=dev,
            device_id_type=pl.DeviceIdType.MESH)

    def face(ph, i, send):
        da, db = DIRS[i]
        if db == 0:
            return (sz if send else hz).at[ph, int(da > 0)]
        if da == 0:
            return (sy if send else hy).at[ph, int(db > 0)]
        return (sc if send else hc).at[ph, 2 * int(da > 0) + int(db > 0)]

    def stage(ph):
        for s in (0, 1):
            sz[ph, s] = C0[0:K, 3 * s].reshape(K * 64, 128).astype(BF16)
            sy[ph, s] = C0[0:K, :, 7 * s].reshape(K * 32, 128).astype(BF16)
            for u in (0, 1):
                sc[ph, 2 * s + u] = C0[0:K, 3 * s, 7 * u].reshape(K * 8, 128).astype(BF16)

    def send_halo(ph):
        for i, (da, db) in enumerate(DIRS):
            @pl.when(exists(da, db))
            def _():
                copy(face(ph, i, True), face(ph, 7 - i, False), hs.at[ph, i], hr.at[ph, 7 - i],
                     beside(da, db)).start()

    def wait_halo(ph):
        for i, (da, db) in enumerate(DIRS):
            @pl.when(exists(da, db))
            def _():
                copy(face(ph, i, True), face(ph, i, False), hs.at[ph, i], hr.at[ph, i],
                     beside(da, db)).wait()
        NZ[:, 0:K] = hz[ph].astype(F32).reshape(2, K, 8, 8, 128)
        NY[:, 0:K] = hy[ph].astype(F32).reshape(2, K, 4, 8, 128)
        NC[:, 0:K] = hc[ph].astype(F32).reshape(4, K, 8, 128)

    def send_coarse(ph):
        for i, (da, db) in enumerate(DIRS):
            @pl.when(exists(da, db))
            def _():
                copy(GA.at[ph, 4], GA.at[ph, 4 - 3 * da - db], cs.at[ph, i], cr.at[ph, 7 - i],
                     beside(da, db)).start()

    def wait_coarse(ph):
        for i, (da, db) in enumerate(DIRS):
            @pl.when(exists(da, db))
            def _():
                copy(GA.at[ph, 4], GA.at[ph, 4 + 3 * da + db], cs.at[ph, i], cr.at[ph, i],
                     beside(da, db)).wait()

    def build():
        xi = lax.broadcasted_iota(jnp.int32, (60, 8, 128), 1)

        def slot(k, carry):
            for e in range(3):
                def at(a, b):
                    v = nb[k, 9 * a + 3 * b + e]
                    return jnp.where(v < 0, K, v)
                FR[e, 1:5, 1:9] = C0[at(1, 1)]
                FR[e, 1:5, 0] = NY[0, at(1, 0)]
                FR[e, 1:5, 9] = NY[1, at(1, 2)]
                FR[e, 0, 1:9] = NZ[0, at(0, 1)]
                FR[e, 5, 1:9] = NZ[1, at(2, 1)]
                FR[e, 0, 0] = NC[0, at(0, 0)]
                FR[e, 0, 9] = NC[1, at(0, 2)]
                FR[e, 5, 0] = NC[2, at(2, 0)]
                FR[e, 5, 9] = NC[3, at(2, 2)]
            mid = FR[1].reshape(60, 8, 128)
            first = pltpu.roll(jnp.where(xi == 7, FR[0].reshape(60, 8, 128), mid), 1, 1)
            last = pltpu.roll(jnp.where(xi == 0, FR[2].reshape(60, 8, 128), mid), 7, 1)
            for e, part in enumerate((first, mid, last)):
                part = part.reshape(6, 10, 8, 128)
                for b in range(3):
                    t = 3 * b + e
                    T[:, k, :, 128 * t:128 * t + 128] = (
                        part[:, b:b + 8].reshape(6, 64, 128).astype(BF16))
            return carry

        lax.fori_loop(0, K, slot, 0)

    C0[0:K] = x_in[...].astype(F32).reshape(K, 4, 8, 8, 128)
    stage(0)
    entered()
    send_halo(0)

    for a in range(3):
        for t in range(9):
            WB[a, 128 * t:128 * t + 128, :] = conv_w[26 - 9 * a - t].astype(F32).T.astype(BF16)
    live = [jnp.where(nb[k, 13] >= 0, 1.0, 0.0).astype(F32) for k in range(K)]
    r_i = lax.broadcasted_iota(jnp.int32, (16, 64), 0)
    c_i = lax.broadcasted_iota(jnp.int32, (16, 64), 1)
    pool = ((r_i // 2 == c_i // 8) & (r_i % 2 == (c_i % 8) // 4)).astype(F32)
    r_j = lax.broadcasted_iota(jnp.int32, (64, 16), 1)
    c_j = lax.broadcasted_iota(jnp.int32, (64, 16), 0)
    unpool = ((r_j // 2 == c_j // 8) & (r_j % 2 == (c_j % 8) // 4)).astype(F32)
    cot_rows = jnp.concatenate(
        [cot_in[k].astype(F32).reshape(4, 2, 4, 8, 128).sum(axis=(0, 2)) * live[k]
         for k in range(K)], axis=0).reshape(64, 128)
    dz = jnp.dot(pool, cot_rows, precision=HIGH, preferred_element_type=F32).astype(BF16)
    grad_q = lax.dot_general(dz, up_w[...], (((1,), (1,)), ((), ())), preferred_element_type=F32)
    pick = (idx_in[...] == lax.broadcasted_iota(jnp.int32, (432, 144), 1)).astype(F32).astype(BF16)
    depth = depth_w[...].astype(F32)
    WF[:, 9] = jnp.zeros((3, 128, 128), F32)

    wait_halo(0)
    build()
    for a in range(3):
        term = jnp.dot(T[a:a + 4].reshape(1024, 1152), conv_w[9 * a:9 * a + 9].reshape(1152, 128),
                       preferred_element_type=F32).reshape(4, K, 64, 128)
        if a == 0:
            FS[...] = term
        else:
            FS[...] += term
    field = FS[...]
    act = field * jax.nn.sigmoid(field)
    act_rows = act.sum(axis=0).reshape(K, 2, 4, 8, 128).sum(axis=2).reshape(64, 128)
    p = jnp.dot(pool, act_rows * (1.0 / 64.0), precision=HIGH, preferred_element_type=F32)
    p = p.astype(BF16)
    g = jnp.dot(p, down_w[...], preferred_element_type=F32).astype(BF16)
    GA[0, 4] = g
    send_coarse(0)
    wait_coarse(0)
    near = jnp.dot(pick, GA[0].reshape(144, 256), preferred_element_type=F32)
    v = jnp.zeros((16, 256), F32)
    for t in range(27):
        v = v + near[16 * t:16 * t + 16] * depth[t:t + 1]
    v = v + g.astype(F32)
    dv = (grad_q * silu_slope(v)).astype(BF16)
    GA[1, 4] = dv
    send_coarse(1)
    dvf = dv.astype(F32)
    q = (v * jax.nn.sigmoid(v)).astype(BF16)
    up_part = lax.dot_general(q, dz, (((0,), (0,)), ((), ())), preferred_element_type=F32)
    DG[...] = jnp.zeros(DG.shape, F32)
    for t in range(27):
        line = jnp.sum(near[16 * t:16 * t + 16] * dvf, axis=0, keepdims=True)
        DG[t:t + 1] = line[:, :128]
        DG[32 + t:33 + t] = line[:, 128:]
    wait_coarse(1)
    near = jnp.dot(pick, GA[1].reshape(144, 256), preferred_element_type=F32)
    dg = jnp.zeros((16, 256), F32)
    for t in range(27):
        u = 26 - t
        dg = dg + near[16 * u:16 * u + 16] * depth[t:t + 1]
    dg = (dg + dvf).astype(BF16)
    dp = lax.dot_general(dg, down_w[...], (((1,), (1,)), ((), ())), preferred_element_type=F32)
    wide = jnp.dot(unpool, dp * (1.0 / 64.0), precision=HIGH, preferred_element_type=F32)
    wide = wide.reshape(K, 2, 8, 128)
    for k in range(K):
        up_rows = cot_in[k].astype(F32).reshape(4, 2, 4, 8, 128) + wide[k].reshape(1, 2, 1, 8, 128)
        slope = silu_slope(FS[:, k]).reshape(4, 2, 4, 8, 128)
        df = (up_rows * slope * live[k]).astype(BF16)
        DF[:, k] = df.reshape(4, 64, 128)
        C0[k] = df.astype(F32).reshape(4, 8, 8, 128)
    stage(1)
    send_halo(1)
    down_part = lax.dot_general(p, dg, (((0,), (0,)), ((), ())), preferred_element_type=F32)

    if reduce:
        sms[:, 0:16] = up_part.reshape(16, 16, 128).astype(BF16)
        sms[0:8, 16:32] = down_part[:, :128].reshape(8, 16, 128).astype(BF16)
        sms[8:16, 16:32] = down_part[:, 128:].reshape(8, 16, 128).astype(BF16)
        sms[0:4, 32:48] = DG[...].reshape(4, 16, 128).astype(BF16)

        def small(r):
            to = lax.rem(me + r, n)
            return copy(sms.at[to], smr.at[me], ss.at[r], sr.at[r], target(to))

        def small_in(r):
            src = lax.rem(me - r + n, n)
            return copy(sms.at[src], smr.at[src], ss.at[r], sr.at[r], target(src))

        def final(r):
            to = lax.rem(me + r, n)
            return copy(ag.at[me], ag.at[me], gs.at[r], gr.at[r], target(to))

        def final_in(r):
            src = lax.rem(me - r + n, n)
            return copy(ag.at[src], ag.at[src], gs.at[r], gr.at[r], target(src))

        def each(count, fn):
            def body(r, carry):
                fn(r)
                return carry
            lax.fori_loop(1, count, body, 0)

        each(n, lambda r: small(r).start())
    else:
        up_out[...] = up_part
        dn_out[...] = down_part
        dp_out[:, :128] = DG[0:27]
        dp_out[:, 128:] = DG[32:59]

    Q = B * S
    mine = blk * S + slab
    other = 1 - ch

    def pair(a):
        return copy(st1.at[a], rv1.at[a], p1s.at[a], p1r.at[a],
                    {"blk": blk, "slab": slab, "ch": other})

    def spread_to(a, r):
        to = lax.rem(mine + r, Q)
        return copy(st2.at[a, to], rv2.at[a, mine], p2s.at[a, r], p2r.at[a, r],
                    {"blk": lax.div(to, S), "slab": lax.rem(to, S), "ch": ch})

    def spread_in(a, r):
        src = lax.rem(mine - r + Q, Q)
        return copy(st2.at[a, src], rv2.at[a, src], p2s.at[a, r], p2r.at[a, r],
                    {"blk": lax.div(src, S), "slab": lax.rem(src, S), "ch": ch})

    def forward_pair(a):
        pair(a).wait()
        for qi in range(Q):
            at = pl.multiple_of(8 * (2 * qi + ch), 8)
            st2[a, qi] = (WF[a, :, pl.ds(at, 8)].reshape(80, 128)
                          + rv1[a, qi].astype(F32)).astype(BF16)
        each(Q, lambda r: spread_to(a, r).start())

    for a in range(3):
        wg = lax.dot_general(T[a:a + 4].reshape(1024, 1152), DF[...].reshape(1024, 128),
                             (((0,), (0,)), ((), ())), preferred_element_type=F32)
        WF[a, 0:9] = wg.reshape(9, 128, 128)
        if reduce:
            for qi in range(Q):
                at = pl.multiple_of(8 * (2 * qi + other), 8)
                st1[a, qi] = WF[a, :, pl.ds(at, 8)].reshape(80, 128).astype(BF16)
            pair(a).start()
            if a > 0:
                forward_pair(a - 1)
        else:
            cw_out[9 * a:9 * a + 9] = wg.reshape(9, 128, 128)
    if reduce:
        each(n, lambda r: small_in(r).wait())
        smr[me] = sms[me]
        total = smr[0].astype(F32)
        for d in range(1, 16):
            total = total + smr[d].astype(F32)
        ag[me] = total.astype(BF16)
        each(n, lambda r: final(r).start())
        forward_pair(2)

    wait_halo(1)
    build()
    for a in range(3):
        term = jnp.dot(T[a:a + 4].reshape(1024, 1152), WB[a],
                       preferred_element_type=F32).reshape(4, K, 64, 128)
        if a == 0:
            FS[...] = term
        else:
            FS[...] += term
    for k in range(K):
        dx_out[k] = FS[:, k].reshape(256, 128).astype(BF16)

    if reduce:
        each(n, lambda r: final_in(r).wait())
        up_out[...] = ag[:, 0:16].astype(F32).reshape(256, 128)
        dn_out[:, :128] = ag[0:8, 16:32].astype(F32).reshape(128, 128)
        dn_out[:, 128:] = ag[8:16, 16:32].astype(F32).reshape(128, 128)
        DG[...] = ag[0:4, 32:48].astype(F32).reshape(64, 128)
        dp_out[:, :128] = DG[0:27]
        dp_out[:, 128:] = DG[32:59]
        for a in range(3):
            each(Q, lambda r: spread_in(a, r).wait())
            rv2[a, mine] = st2[a, mine]
            total = rv2[a, 0].astype(F32)
            for qi in range(1, 8):
                total = total + rv2[a, qi].astype(F32)
            cw_out[9 * a:9 * a + 9] = total.reshape(10, 8, 128)[0:9]


def coarse_sources():
    block = np.zeros((27, 4), np.int32)
    base = np.zeros((27, 4), np.int32)
    for t in range(27):
        a, b, e = t // 9, t // 3 % 3, t % 3
        for c in range(4):
            y, x = c // 2 + b - 1, c % 2 + e - 1
            by, bx = y // 2 + 1, x // 2 + 1
            block[t, c] = 9 * a + 3 * by + bx
            base[t, c] = (3 * a + by) * 16 + (y % 2) * 2 + x % 2
    return block, base


def per_device(
    mesh_sizes, fine_input, cotangent, conv_weight, down_weight, depth_weight, up_weight, slot_x, neighbours
):
    B, S, H = mesh_sizes
    n = B * S * H
    reduce = n == 16 and H == 2
    nb = neighbours[0, 0]
    block, base = coarse_sources()
    hit = jnp.asarray(block)[:, None, :, None] == jnp.arange(27, dtype=jnp.int32)
    found = jnp.sum(jnp.where(hit, nb[None, :, None, :], 0), axis=-1)
    idx = jnp.where(found >= 0, jnp.asarray(base)[:, None, :] + 4 * found, -1).reshape(432, 1)
    vm = pl.BlockSpec(memory_space=pltpu.VMEM)
    sm = pl.BlockSpec(memory_space=pltpu.SMEM)
    dma = pltpu.SemaphoreType.DMA
    V = pltpu.VMEM
    wide_rows = 8 if reduce else 128
    outs = pl.pallas_call(
        functools.partial(level_kernel, mesh_sizes, reduce),
        out_shape=(
            jax.ShapeDtypeStruct((4, 256, 128), BF16),
            jax.ShapeDtypeStruct((27, wide_rows, 128), F32),
            jax.ShapeDtypeStruct((128, 256), F32),
            jax.ShapeDtypeStruct((27, 256), F32),
            jax.ShapeDtypeStruct((256, 128), F32),
        ),
        in_specs=[sm] + [vm] * 7,
        out_specs=(vm,) * 5,
        scratch_shapes=[
            V((5, 4, 8, 8, 128), F32), V((2, 5, 8, 8, 128), F32), V((2, 5, 4, 8, 128), F32),
            V((4, 5, 8, 128), F32),
            V((2, 2, 256, 128), BF16), V((2, 2, 128, 128), BF16), V((2, 4, 32, 128), BF16),
            V((2, 2, 256, 128), BF16), V((2, 2, 128, 128), BF16), V((2, 4, 32, 128), BF16),
            V((3, 6, 10, 8, 128), F32), V((6, 4, 64, 1152), BF16), V((4, 4, 64, 128), F32),
            V((4, 4, 64, 128), BF16), V((3, 1152, 128), BF16), V((2, 9, 16, 256), BF16),
            V((3, 10, 128, 128), F32),
            V((3, 8, 80, 128), BF16), V((3, 8, 80, 128), BF16),
            V((3, 8, 80, 128), BF16), V((3, 8, 80, 128), BF16),
            V((16, 48, 128), BF16), V((16, 48, 128), BF16), V((16, 48, 128), BF16),
            V((64, 128), F32),
            dma((2, 8)), dma((2, 8)), dma((2, 8)), dma((2, 8)),
            dma((3,)), dma((3,)), dma((3, 8)), dma((3, 8)),
            dma((16,)), dma((16,)), dma((16,)), dma((16,)),
        ],
        compiler_params=pltpu.CompilerParams(
            collective_id=0, has_side_effects=True, vmem_limit_bytes=48 * 1024 * 1024),
        name="level_pair",
    )(nb, fine_input[0, 0], cotangent[0, 0], conv_weight, down_weight, depth_weight, up_weight, idx)
    dx, cw, dn, dp, up = outs
    dx = dx.reshape(fine_input.shape)
    if reduce:
        cw = cw.reshape(27, 1024)
    else:
        axes = ("blk", "slab", "ch")
        dn, dp, up = lax.psum((dn, dp, up), axes)
        cw = lax.psum_scatter(cw.reshape(27, 128 * 128), axes, scatter_dimension=1, tiled=True)
    return dx, cw, dn, dp, up


def solution(mesh):
    sizes = (mesh.shape["blk"], mesh.shape["slab"], mesh.shape["ch"])
    fine = P(("groups", "slab", "ch"), "blk", None, None, None)
    in_specs = (
        fine, fine, P(), P(), P(), P(),
        P(("groups", "slab", "ch"), "blk", None),
        P(("groups", "slab", "ch"), "blk", None, None),
    )
    out_specs = (
        fine,
        P("groups", ("blk", "slab", "ch")),
        P("groups", None),
        P("groups", None),
        P("groups", None),
    )
    return jax.shard_map(
        functools.partial(per_device, sizes), mesh=mesh, in_specs=in_specs, out_specs=out_specs,
        check_vma=False)
```

```python
import functools

import jax
import jax.numpy as jnp
from jax import lax
from jax.experimental import pallas as pl
from jax.experimental.pallas import tpu as pltpu
from jax.sharding import PartitionSpec as P

F32 = jnp.float32
BF16 = jnp.bfloat16
HIGH = lax.Precision.HIGHEST
DIRS = [(da, db) for da in (-1, 0, 1) for db in (-1, 0, 1) if (da, db) != (0, 0)]


def silu_slope(value):
    sigma = jax.nn.sigmoid(value)
    return sigma * (1.0 + value * (1.0 - sigma))


def level_kernel(
    sizes, reduce, nb, nbv, depth_w, x_hbm, cot_hbm, conv_hbm, down_hbm, up_hbm,
    dx_out, cw_out, dn_out, dp_out, up_out,
    C0, NZ, NY, NC, hz, hy, hc, sz, sy, sc, FR, T, FS, DF, WB, GA, WF,
    st10, st11, st12, rv10, rv11, rv12, st20, st21, st22, rv20, rv21, rv22,
    st30, st31, st32, rv30, rv31, rv32, ag, DG, SMALL, x_in, cot_in, conv_w, down_w, up_w,
    hs, hr, cs, cr, p1s, p1r, p2s, p2r, p3s, p3r, gs, gr, ls,
):
    B, S, H = sizes
    K = 4
    blk, slab, ch = lax.axis_index("blk"), lax.axis_index("slab"), lax.axis_index("ch")
    row = slab * H + ch
    rows = S * H
    n = B * S * H
    me = blk * rows + row

    def target(d):
        return {"blk": lax.div(d, rows), "slab": lax.rem(lax.div(d, H), S), "ch": lax.rem(d, H)}

    def exists(da, db):
        r, c = row + da, blk + db
        return (r >= 0) & (r < rows) & (c >= 0) & (c < B)

    def beside(da, db):
        return target((blk + db) * rows + row + da)

    pulls = [pltpu.make_async_copy(src, dst, ls.at[i]) for i, (src, dst) in enumerate((
        (x_hbm, x_in), (cot_hbm, cot_in), (conv_hbm, conv_w), (up_hbm, up_w), (down_hbm, down_w)))]
    for pull in pulls:
        pull.start()

    for ref in (hz, hy, hc, GA):
        ref[...] = jnp.zeros(ref.shape, ref.dtype)
    C0[K] = jnp.zeros(C0.shape[1:], F32)
    NZ[:, K] = jnp.zeros((2,) + NZ.shape[2:], F32)
    NY[:, K] = jnp.zeros((2,) + NY.shape[2:], F32)
    NC[:, K] = jnp.zeros((4,) + NC.shape[2:], F32)
    barrier = pltpu.get_barrier_semaphore()
    if reduce:
        def greet(r, carry):
            pl.semaphore_signal(barrier, inc=1, device_id=target(lax.rem(me + r, n)),
                                device_id_type=pl.DeviceIdType.MESH)
            return carry
        lax.fori_loop(1, n, greet, 0)
    else:
        for da, db in DIRS:
            @pl.when(exists(da, db))
            def _():
                pl.semaphore_signal(barrier, inc=1, device_id=beside(da, db),
                                    device_id_type=pl.DeviceIdType.MESH)

    def entered():
        if reduce:
            pl.semaphore_wait(barrier, n - 1)
        else:
            for da, db in DIRS:
                @pl.when(exists(da, db))
                def _():
                    pl.semaphore_wait(barrier, 1)

    def copy(src, dst, s, r, dev):
        return pltpu.make_async_remote_copy(
            src_ref=src, dst_ref=dst, send_sem=s, recv_sem=r, device_id=dev,
            device_id_type=pl.DeviceIdType.MESH)

    def face(ph, i, send):
        da, db = DIRS[i]
        if db == 0:
            return (sz if send else hz).at[ph, int(da > 0)]
        if da == 0:
            return (sy if send else hy).at[ph, int(db > 0)]
        return (sc if send else hc).at[ph, 2 * int(da > 0) + int(db > 0)]

    def stage(ph):
        for s in (0, 1):
            sz[ph, s] = C0[0:K, 3 * s].reshape(K * 64, 128).astype(BF16)
            sy[ph, s] = C0[0:K, :, 7 * s].reshape(K * 32, 128).astype(BF16)
            for u in (0, 1):
                sc[ph, 2 * s + u] = C0[0:K, 3 * s, 7 * u].reshape(K * 8, 128).astype(BF16)

    def send_halo(ph):
        for i, (da, db) in enumerate(DIRS):
            @pl.when(exists(da, db))
            def _():
                copy(face(ph, i, True), face(ph, 7 - i, False), hs.at[ph, i], hr.at[ph, 7 - i],
                     beside(da, db)).start()

    def wait_halo(ph):
        for i, (da, db) in enumerate(DIRS):
            @pl.when(exists(da, db))
            def _():
                copy(face(ph, i, True), face(ph, i, False), hs.at[ph, i], hr.at[ph, i],
                     beside(da, db)).wait()
        NZ[:, 0:K] = hz[ph].astype(F32).reshape(2, K, 8, 8, 128)
        NY[:, 0:K] = hy[ph].astype(F32).reshape(2, K, 4, 8, 128)
        NC[:, 0:K] = hc[ph].astype(F32).reshape(4, K, 8, 128)

    def send_coarse(ph):
        for i, (da, db) in enumerate(DIRS):
            @pl.when(exists(da, db))
            def _():
                copy(GA.at[ph, 4], GA.at[ph, 4 - 3 * da - db], cs.at[ph, i], cr.at[ph, 7 - i],
                     beside(da, db)).start()

    def wait_coarse(ph):
        for i, (da, db) in enumerate(DIRS):
            @pl.when(exists(da, db))
            def _():
                copy(GA.at[ph, 4], GA.at[ph, 4 + 3 * da + db], cs.at[ph, i], cr.at[ph, i],
                     beside(da, db)).wait()

    def build():
        xi = lax.broadcasted_iota(jnp.int32, (60, 8, 128), 1)

        def slot(k, carry):
            for e in range(3):
                def at(a, b):
                    v = nb[k, 9 * a + 3 * b + e]
                    return jnp.where(v < 0, K, v)
                FR[e, 1:5, 1:9] = C0[at(1, 1)]
                FR[e, 1:5, 0] = NY[0, at(1, 0)]
                FR[e, 1:5, 9] = NY[1, at(1, 2)]
                FR[e, 0, 1:9] = NZ[0, at(0, 1)]
                FR[e, 5, 1:9] = NZ[1, at(2, 1)]
                FR[e, 0, 0] = NC[0, at(0, 0)]
                FR[e, 0, 9] = NC[1, at(0, 2)]
                FR[e, 5, 0] = NC[2, at(2, 0)]
                FR[e, 5, 9] = NC[3, at(2, 2)]
            mid = FR[1].reshape(60, 8, 128)
            first = pltpu.roll(jnp.where(xi == 7, FR[0].reshape(60, 8, 128), mid), 1, 1)
            last = pltpu.roll(jnp.where(xi == 0, FR[2].reshape(60, 8, 128), mid), 7, 1)
            for e, part in enumerate((first, mid, last)):
                part = part.reshape(6, 10, 8, 128)
                for b in range(3):
                    t = 3 * b + e
                    T[:, k, :, 128 * t:128 * t + 128] = (
                        part[:, b:b + 8].reshape(6, 64, 128).astype(BF16))
            return carry

        lax.fori_loop(0, K, slot, 0)

    pulls[0].wait()
    C0[0:K] = x_in[...].astype(F32).reshape(K, 4, 8, 8, 128)
    stage(0)
    entered()
    send_halo(0)

    for pull in pulls[1:]:
        pull.wait()
    for a in range(3):
        for t in range(9):
            WB[a, 128 * t:128 * t + 128, :] = conv_w[26 - 9 * a - t].astype(F32).T.astype(BF16)
    live = [jnp.where(nb[k, 13] >= 0, 1.0, 0.0).astype(F32) for k in range(K)]
    r_i = lax.broadcasted_iota(jnp.int32, (16, 64), 0)
    c_i = lax.broadcasted_iota(jnp.int32, (16, 64), 1)
    pool = ((r_i // 2 == c_i // 8) & (r_i % 2 == (c_i % 8) // 4)).astype(F32)
    r_j = lax.broadcasted_iota(jnp.int32, (64, 16), 1)
    c_j = lax.broadcasted_iota(jnp.int32, (64, 16), 0)
    unpool = ((r_j // 2 == c_j // 8) & (r_j % 2 == (c_j % 8) // 4)).astype(F32)
    cot_rows = jnp.concatenate(
        [cot_in[k].astype(F32).reshape(4, 2, 4, 8, 128).sum(axis=(0, 2)) * live[k]
         for k in range(K)], axis=0).reshape(64, 128)
    dz = jnp.dot(pool, cot_rows, precision=HIGH, preferred_element_type=F32).astype(BF16)
    grad_q = lax.dot_general(dz, up_w[...], (((1,), (1,)), ((), ())), preferred_element_type=F32)
    depth = jnp.concatenate([depth_w[...].astype(F32), jnp.zeros((5, 256), F32)], axis=0)
    turn_r = lax.broadcasted_iota(jnp.int32, (32, 32), 0)
    turn_c = lax.broadcasted_iota(jnp.int32, (32, 32), 1)
    turned = jnp.dot((turn_r + turn_c == 26).astype(F32), depth, precision=HIGH,
                     preferred_element_type=F32)

    def source(c, shape):
        t = lax.broadcasted_iota(jnp.int32, shape, 0)
        ys, xs = t // 3 % 3 + c // 2 + 1, t % 3 + c % 2 + 1
        block = 9 * (t // 9) + 3 * (ys // 2) + xs // 2
        base = (3 * (t // 9) + ys // 2) * 16 + ys % 2 * 2 + xs % 2
        return t, block, base

    found = []
    for c in range(4):
        t, block, _ = source(c, (32, 27))
        hit = ((block == lax.broadcasted_iota(jnp.int32, (32, 27), 1)) & (t < 27)).astype(F32)
        found.append(lax.dot_general(hit, nbv[...].astype(F32), (((1,), (1,)), ((), ())),
                                     precision=HIGH, preferred_element_type=F32))
    picks = []
    for k in range(K):
        for c in range(4):
            t, _, base = source(c, (32, 144))
            col = (lax.broadcasted_iota(jnp.int32, (32, 144), 1) - base).astype(F32)
            slot_of = found[c][:, k:k + 1]
            picks.append(((col == 4.0 * slot_of) & (slot_of >= 0.0) & (t < 27)).astype(F32))
    pick = jnp.concatenate(picks, axis=0).astype(BF16)
    WF[:, 9] = jnp.zeros((3, 128, 128), F32)

    wait_halo(0)
    build()
    for a in range(3):
        term = jnp.dot(T[a:a + 4].reshape(1024, 1152), conv_w[9 * a:9 * a + 9].reshape(1152, 128),
                       preferred_element_type=F32).reshape(4, K, 64, 128)
        if a == 0:
            FS[...] = term
        else:
            FS[...] += term
    field = FS[...]
    act = field * jax.nn.sigmoid(field)
    act_rows = act.sum(axis=0).reshape(K, 2, 4, 8, 128).sum(axis=2).reshape(64, 128)
    p = jnp.dot(pool, act_rows * (1.0 / 64.0), precision=HIGH, preferred_element_type=F32)
    p = p.astype(BF16)
    g = jnp.dot(p, down_w[...], preferred_element_type=F32).astype(BF16)
    GA[0, 4] = g
    send_coarse(0)
    wait_coarse(0)
    near = jnp.dot(pick, GA[0].reshape(144, 256), preferred_element_type=F32).reshape(16, 32, 256)
    v = g.astype(F32) + jnp.sum(near * depth[None], axis=1)
    dv = (grad_q * silu_slope(v)).astype(BF16)
    GA[1, 4] = dv
    send_coarse(1)
    dvf = dv.astype(F32)
    q = (v * jax.nn.sigmoid(v)).astype(BF16)
    up_part = lax.dot_general(q, dz, (((0,), (0,)), ((), ())), preferred_element_type=F32)
    lines = near[0] * dvf[0:1]
    for c in range(1, 16):
        lines = lines + near[c] * dvf[c:c + 1]
    DG[0:32] = lines[:, :128]
    DG[32:64] = lines[:, 128:]
    wait_coarse(1)
    near = jnp.dot(pick, GA[1].reshape(144, 256), preferred_element_type=F32).reshape(16, 32, 256)
    dg = (jnp.sum(near * turned[None], axis=1) + dvf).astype(BF16)
    dp = lax.dot_general(dg, down_w[...], (((1,), (1,)), ((), ())), preferred_element_type=F32)
    wide = jnp.dot(unpool, dp * (1.0 / 64.0), precision=HIGH, preferred_element_type=F32)
    wide = wide.reshape(K, 2, 8, 128)
    for k in range(K):
        up_rows = cot_in[k].astype(F32).reshape(4, 2, 4, 8, 128) + wide[k].reshape(1, 2, 1, 8, 128)
        slope = silu_slope(FS[:, k]).reshape(4, 2, 4, 8, 128)
        df = (up_rows * slope * live[k]).astype(BF16)
        DF[:, k] = df.reshape(4, 64, 128)
        C0[k] = df.astype(F32).reshape(4, 8, 8, 128)
    stage(1)
    send_halo(1)
    down_part = lax.dot_general(p, dg, (((0,), (0,)), ((), ())), preferred_element_type=F32)

    st1, rv1 = (st10, st11, st12), (rv10, rv11, rv12)
    st2, rv2 = (st20, st21, st22), (rv20, rv21, rv22)
    st3, rv3 = (st30, st31, st32), (rv30, rv31, rv32)
    Q = B * S
    mine = blk * S + slab

    def each(count, fn):
        def body(r, carry):
            fn(r)
            return carry
        lax.fori_loop(1, count, body, 0)

    def at_chip(q):
        return {"blk": lax.div(q, S), "slab": lax.rem(q, S), "ch": ch}

    def across(a):
        return copy(st1[a], rv1[a], p1s.at[a], p1r.at[a],
                    {"blk": blk, "slab": slab, "ch": 1 - ch})

    def along_slab(a):
        return copy(st2[a].at[1 - slab], rv2[a], p2s.at[a], p2r.at[a],
                    {"blk": blk, "slab": 1 - slab, "ch": ch})

    def along_blk(a, r):
        to = lax.rem(blk + r, B)
        return copy(st3[a].at[to], rv3[a].at[blk], p3s.at[a, r], p3r.at[a, r],
                    {"blk": to, "slab": slab, "ch": ch})

    def from_blk(a, r):
        src = lax.rem(blk - r + B, B)
        return copy(st3[a].at[src], rv3[a].at[src], p3s.at[a, r], p3r.at[a, r],
                    {"blk": src, "slab": slab, "ch": ch})

    def gather_out(r):
        to = lax.rem(mine + r, Q)
        return copy(ag.at[ch, mine], ag.at[ch, mine], gs.at[r], gr.at[r], at_chip(to))

    def gather_in(r):
        src = lax.rem(mine - r + Q, Q)
        return copy(ag.at[ch, src], ag.at[ch, src], gs.at[r], gr.at[r], at_chip(src))

    def gather_pair(side):
        return copy(ag.at[side], ag.at[side], gs.at[0], gr.at[0],
                    {"blk": blk, "slab": slab, "ch": 1 - ch})

    def step_core(a):
        for sl in range(S):
            for bk in range(B):
                at = pl.multiple_of(8 * ((bk * S + sl) * 2 + 1 - ch), 8)
                st1[a][sl, bk, 0:80] = WF[a, :, pl.ds(at, 8)].reshape(80, 128).astype(BF16)
        across(a).start()

    def step_slab(a):
        across(a).wait()
        for sl in range(S):
            for bk in range(B):
                at = pl.multiple_of(8 * ((bk * S + sl) * 2 + ch), 8)
                st2[a][sl, bk, 0:80] = (WF[a, :, pl.ds(at, 8)].reshape(80, 128)
                                        + rv1[a][sl, bk, 0:80].astype(F32)).astype(BF16)
                if a == 0:
                    st2[a][sl, bk, 80:128] = (SMALL[2 * (bk * S + sl) + ch]
                                              + rv1[a][sl, bk, 80:128].astype(F32)).astype(BF16)
        along_slab(a).start()

    def step_blk(a):
        along_slab(a).wait()
        st3[a][...] = (st2[a][slab].astype(F32) + rv2[a][...].astype(F32)).astype(BF16)
        each(B, lambda r: along_blk(a, r).start())

    def step_sum(a):
        each(B, lambda r: from_blk(a, r).wait())
        rv3[a][blk] = st3[a][blk]
        total = rv3[a][0].astype(F32)
        for bk in range(1, B):
            total = total + rv3[a][bk].astype(F32)
        cw_out[9 * a:9 * a + 9] = total[0:80].reshape(10, 8, 128)[0:9]
        return total

    if reduce:
        SMALL[:, 0:16] = up_part.reshape(16, 16, 128)
        SMALL[0:8, 16:32] = down_part[:, :128].reshape(8, 16, 128)
        SMALL[8:16, 16:32] = down_part[:, 128:].reshape(8, 16, 128)
        SMALL[0:4, 32:48] = DG[...].reshape(4, 16, 128)
        SMALL[4:16, 32:48] = jnp.zeros((12, 16, 128), F32)
        for sl in range(S):
            for bk in range(B):
                st10[sl, bk, 80:128] = SMALL[2 * (bk * S + sl) + 1 - ch].astype(BF16)
    else:
        up_out[...] = up_part
        dn_out[...] = down_part
        dp_out[:, :128] = DG[0:27]
        dp_out[:, 128:] = DG[32:59]

    for a in range(3):
        wg = lax.dot_general(T[a:a + 4].reshape(1024, 1152), DF[...].reshape(1024, 128),
                             (((0,), (0,)), ((), ())), preferred_element_type=F32)
        if reduce:
            WF[a, 0:9] = wg.reshape(9, 128, 128)
            step_core(a)
            if a > 0:
                step_slab(a - 1)
            if a > 1:
                step_blk(a - 2)
        else:
            cw_out[9 * a:9 * a + 9] = wg.reshape(9, 128, 128)
    if reduce:
        step_slab(2)
        step_blk(1)

    wait_halo(1)
    build()
    if reduce:
        step_blk(2)
        ag[ch, mine] = step_sum(0)[80:128].astype(BF16)
        each(Q, lambda r: gather_out(r).start())
    for a in range(3):
        term = jnp.dot(T[a:a + 4].reshape(1024, 1152), WB[a],
                       preferred_element_type=F32).reshape(4, K, 64, 128)
        if a == 0:
            FS[...] = term
        else:
            FS[...] += term
    for k in range(K):
        dx_out[k] = FS[:, k].reshape(256, 128).astype(BF16)

    if reduce:
        step_sum(1)
        each(Q, lambda r: gather_in(r).wait())
        gather_pair(ch).start()
        step_sum(2)
        gather_pair(1 - ch).wait()
        for c in range(2):
            for qi in range(8):
                d = 2 * qi + c
                up_out[16 * d:16 * d + 16] = ag[c, qi, 0:16].astype(F32)
                at, side = 16 * (d % 8), 128 * (d // 8)
                dn_out[at:at + 16, side:side + 128] = ag[c, qi, 16:32].astype(F32)
                if d < 4:
                    DG[16 * d:16 * d + 16] = ag[c, qi, 32:48].astype(F32)
        dp_out[:, :128] = DG[0:27]
        dp_out[:, 128:] = DG[32:59]


def write_kernel(dx, cw, dn, dp, up, dx_o, cw_o, dn_o, dp_o, up_o, flat, sem):
    moves = [pltpu.make_async_copy(src, dst, sem.at[i])
             for i, (src, dst) in enumerate(((dx, dx_o), (dn, dn_o), (dp, dp_o), (up, up_o)))]
    for move in moves:
        move.start()
    for i in range(8):
        flat[:, 128 * i:128 * i + 128] = cw[:, i, :]
    moves.append(pltpu.make_async_copy(flat, cw_o, sem.at[4]))
    moves[4].start()
    for move in moves:
        move.wait()


def per_device(
    mesh_sizes, fine_input, cotangent, conv_weight, down_weight, depth_weight, up_weight, slot_x, neighbours
):
    B, S, H = mesh_sizes
    n = B * S * H
    reduce = (B, S, H) == (4, 2, 2)
    nb = neighbours[0, 0]
    vm = pl.BlockSpec(memory_space=pltpu.VMEM)
    sm = pl.BlockSpec(memory_space=pltpu.SMEM)
    dma = pltpu.SemaphoreType.DMA
    V = pltpu.VMEM
    wide_rows = 8 if reduce else 128
    part_rows = (128, 80, 80)
    outs = pl.pallas_call(
        functools.partial(level_kernel, mesh_sizes, reduce),
        out_shape=(
            jax.ShapeDtypeStruct((4, 256, 128), BF16),
            jax.ShapeDtypeStruct((27, wide_rows, 128), F32),
            jax.ShapeDtypeStruct((128, 256), F32),
            jax.ShapeDtypeStruct((27, 256), F32),
            jax.ShapeDtypeStruct((256, 128), F32),
        ),
        in_specs=[sm, vm, vm] + [pl.BlockSpec(memory_space=pl.ANY)] * 5,
        out_specs=(vm,) * 5,
        scratch_shapes=[
            V((5, 4, 8, 8, 128), F32), V((2, 5, 8, 8, 128), F32), V((2, 5, 4, 8, 128), F32),
            V((4, 5, 8, 128), F32),
            V((2, 2, 256, 128), BF16), V((2, 2, 128, 128), BF16), V((2, 4, 32, 128), BF16),
            V((2, 2, 256, 128), BF16), V((2, 2, 128, 128), BF16), V((2, 4, 32, 128), BF16),
            V((3, 6, 10, 8, 128), F32), V((6, 4, 64, 1152), BF16), V((4, 4, 64, 128), F32),
            V((4, 4, 64, 128), BF16), V((3, 1152, 128), BF16), V((2, 9, 16, 256), BF16),
            V((3, 10, 128, 128), F32),
            *[V((2, B, rows, 128), BF16) for rows in part_rows],
            *[V((2, B, rows, 128), BF16) for rows in part_rows],
            *[V((2, B, rows, 128), BF16) for rows in part_rows],
            *[V((B, rows, 128), BF16) for rows in part_rows],
            *[V((B, rows, 128), BF16) for rows in part_rows],
            *[V((B, rows, 128), BF16) for rows in part_rows],
            V((2, 8, 48, 128), BF16),
            V((64, 128), F32), V((16, 48, 128), F32),
            V((4, 256, 128), BF16), V((4, 256, 128), BF16), V((27, 128, 128), BF16),
            V((128, 256), BF16), V((256, 128), BF16),
            dma((2, 8)), dma((2, 8)), dma((2, 8)), dma((2, 8)),
            dma((3,)), dma((3,)), dma((3,)), dma((3,)), dma((3, 4)), dma((3, 4)),
            dma((8,)), dma((8,)), dma((5,)),
        ],
        compiler_params=pltpu.CompilerParams(
            collective_id=0, has_side_effects=True, vmem_limit_bytes=48 * 1024 * 1024),
        name="level_pair",
    )(nb, nb, depth_weight, fine_input[0, 0], cotangent[0, 0], conv_weight, down_weight, up_weight)
    dx, cw, dn, dp, up = outs
    if reduce:
        hbm = pl.BlockSpec(memory_space=pl.ANY)
        dx, cw, dn, dp, up = pl.pallas_call(
            write_kernel,
            out_shape=(dx, jax.ShapeDtypeStruct((27, 1024), F32), dn, dp, up),
            in_specs=[vm] * 5,
            out_specs=(hbm,) * 5,
            scratch_shapes=[V((27, 1024), F32), dma((5,))],
            name="write_out",
        )(dx, cw, dn, dp, up)
    else:
        axes = ("blk", "slab", "ch")
        dn, dp, up = lax.psum((dn, dp, up), axes)
        cw = lax.psum_scatter(cw.reshape(27, 128 * 128), axes, scatter_dimension=1, tiled=True)
    return dx.reshape(fine_input.shape), cw, dn, dp, up


def solution(mesh):
    sizes = (mesh.shape["blk"], mesh.shape["slab"], mesh.shape["ch"])
    fine = P(("groups", "slab", "ch"), "blk", None, None, None)
    in_specs = (
        fine, fine, P(), P(), P(), P(),
        P(("groups", "slab", "ch"), "blk", None),
        P(("groups", "slab", "ch"), "blk", None, None),
    )
    out_specs = (
        fine,
        P("groups", ("blk", "slab", "ch")),
        P("groups", None),
        P("groups", None),
        P("groups", None),
    )
    return jax.shard_map(
        functools.partial(per_device, sizes), mesh=mesh, in_specs=in_specs, out_specs=out_specs,
        check_vma=False)
```

```python
import functools

import jax
import jax.numpy as jnp
from jax import lax
from jax.experimental import pallas as pl
from jax.experimental.pallas import tpu as pltpu
from jax.sharding import PartitionSpec as P

F32 = jnp.float32
BF16 = jnp.bfloat16
GRANT = 64 * 1024 * 1024 - 128 * 1024
HIGH = lax.Precision.HIGHEST
DIRS = [(da, db) for da in (-1, 0, 1) for db in (-1, 0, 1) if (da, db) != (0, 0)]


def silu_slope(value):
    sigma = jax.nn.sigmoid(value)
    return sigma * (1.0 + value * (1.0 - sigma))


def level_kernel(
    sizes, reduce, nb_hbm, depth_hbm, x_hbm, cot_hbm, conv_hbm, down_hbm, up_hbm,
    dx_hbm, cw_hbm, dn_hbm, dp_hbm, up_out_hbm,
    C0, NZ, NY, NC, hz, hy, hc, sz, sy, sc, FR, T, FS, DF, WB, GA, WF,
    st10, st11, st12, rv10, rv11, rv12, st20, st21, st22, rv20, rv21, rv22,
    st30, st31, st32, rv30, rv31, rv32, ag, DG, SMALL, x_in, cot_in, conv_w, down_w, up_w,
    nb, nbv, depth_w, dx_out, cw_out, dn_out, dp_out, up_out,
    hs, hr, cs, cr, p1s, p1r, p2s, p2r, p3s, p3r, gs, gr, ls, os,
):
    B, S, H = sizes
    K = 4
    blk, slab, ch = lax.axis_index("blk"), lax.axis_index("slab"), lax.axis_index("ch")
    row = slab * H + ch
    rows = S * H
    n = B * S * H
    me = blk * rows + row

    def target(d):
        return {"blk": lax.div(d, rows), "slab": lax.rem(lax.div(d, H), S), "ch": lax.rem(d, H)}

    def exists(da, db):
        r, c = row + da, blk + db
        return (r >= 0) & (r < rows) & (c >= 0) & (c < B)

    def beside(da, db):
        return target((blk + db) * rows + row + da)

    pulls = [pltpu.make_async_copy(src, dst, ls.at[i]) for i, (src, dst) in enumerate((
        (x_hbm, x_in), (cot_hbm, cot_in), (nb_hbm, nb), (nb_hbm, nbv), (depth_hbm, depth_w),
        (up_hbm, up_w), (down_hbm, down_w), (conv_hbm, conv_w)))]
    pushes = [pltpu.make_async_copy(src, dst, os.at[i]) for i, (src, dst) in enumerate((
        (dx_out, dx_hbm), (cw_out, cw_hbm), (dn_out, dn_hbm), (dp_out, dp_hbm), (up_out, up_out_hbm)))]
    for pull in pulls:
        pull.start()

    for ref in (hz, hy, hc, GA):
        ref[...] = jnp.zeros(ref.shape, ref.dtype)
    C0[K] = jnp.zeros(C0.shape[1:], F32)
    NZ[:, K] = jnp.zeros((2,) + NZ.shape[2:], F32)
    NY[:, K] = jnp.zeros((2,) + NY.shape[2:], F32)
    NC[:, K] = jnp.zeros((4,) + NC.shape[2:], F32)
    barrier = pltpu.get_barrier_semaphore()
    if reduce:
        def greet(r, carry):
            pl.semaphore_signal(barrier, inc=1, device_id=target(lax.rem(me + r, n)),
                                device_id_type=pl.DeviceIdType.MESH)
            return carry
        lax.fori_loop(1, n, greet, 0)
    else:
        for da, db in DIRS:
            @pl.when(exists(da, db))
            def _():
                pl.semaphore_signal(barrier, inc=1, device_id=beside(da, db),
                                    device_id_type=pl.DeviceIdType.MESH)

    def entered():
        if reduce:
            pl.semaphore_wait(barrier, n - 1)
        else:
            for da, db in DIRS:
                @pl.when(exists(da, db))
                def _():
                    pl.semaphore_wait(barrier, 1)

    def copy(src, dst, s, r, dev):
        return pltpu.make_async_remote_copy(
            src_ref=src, dst_ref=dst, send_sem=s, recv_sem=r, device_id=dev,
            device_id_type=pl.DeviceIdType.MESH)

    def face(ph, i, send):
        da, db = DIRS[i]
        if db == 0:
            return (sz if send else hz).at[ph, int(da > 0)]
        if da == 0:
            return (sy if send else hy).at[ph, int(db > 0)]
        return (sc if send else hc).at[ph, 2 * int(da > 0) + int(db > 0)]

    def stage(ph):
        for s in (0, 1):
            sz[ph, s] = C0[0:K, 3 * s].reshape(K * 64, 128).astype(BF16)
            sy[ph, s] = C0[0:K, :, 7 * s].reshape(K * 32, 128).astype(BF16)
            for u in (0, 1):
                sc[ph, 2 * s + u] = C0[0:K, 3 * s, 7 * u].reshape(K * 8, 128).astype(BF16)

    def send_halo(ph):
        for i, (da, db) in enumerate(DIRS):
            @pl.when(exists(da, db))
            def _():
                copy(face(ph, i, True), face(ph, 7 - i, False), hs.at[ph, i], hr.at[ph, 7 - i],
                     beside(da, db)).start()

    def wait_halo(ph):
        for i, (da, db) in enumerate(DIRS):
            @pl.when(exists(da, db))
            def _():
                copy(face(ph, i, True), face(ph, i, False), hs.at[ph, i], hr.at[ph, i],
                     beside(da, db)).wait()
        NZ[:, 0:K] = hz[ph].astype(F32).reshape(2, K, 8, 8, 128)
        NY[:, 0:K] = hy[ph].astype(F32).reshape(2, K, 4, 8, 128)
        NC[:, 0:K] = hc[ph].astype(F32).reshape(4, K, 8, 128)

    def send_coarse(ph):
        for i, (da, db) in enumerate(DIRS):
            @pl.when(exists(da, db))
            def _():
                copy(GA.at[ph, 4], GA.at[ph, 4 - 3 * da - db], cs.at[ph, i], cr.at[ph, 7 - i],
                     beside(da, db)).start()

    def wait_coarse(ph):
        for i, (da, db) in enumerate(DIRS):
            @pl.when(exists(da, db))
            def _():
                copy(GA.at[ph, 4], GA.at[ph, 4 + 3 * da + db], cs.at[ph, i], cr.at[ph, i],
                     beside(da, db)).wait()

    def build():
        xi = lax.broadcasted_iota(jnp.int32, (60, 8, 128), 1)

        def slot(k, carry):
            for e in range(3):
                def at(a, b):
                    v = nb[k, 9 * a + 3 * b + e]
                    return jnp.where(v < 0, K, v)
                FR[e, 1:5, 1:9] = C0[at(1, 1)]
                FR[e, 1:5, 0] = NY[0, at(1, 0)]
                FR[e, 1:5, 9] = NY[1, at(1, 2)]
                FR[e, 0, 1:9] = NZ[0, at(0, 1)]
                FR[e, 5, 1:9] = NZ[1, at(2, 1)]
                FR[e, 0, 0] = NC[0, at(0, 0)]
                FR[e, 0, 9] = NC[1, at(0, 2)]
                FR[e, 5, 0] = NC[2, at(2, 0)]
                FR[e, 5, 9] = NC[3, at(2, 2)]
            mid = FR[1].reshape(60, 8, 128)
            first = pltpu.roll(jnp.where(xi == 7, FR[0].reshape(60, 8, 128), mid), 1, 1)
            last = pltpu.roll(jnp.where(xi == 0, FR[2].reshape(60, 8, 128), mid), 7, 1)
            for e, part in enumerate((first, mid, last)):
                part = part.reshape(6, 10, 8, 128)
                for b in range(3):
                    t = 3 * b + e
                    T[:, k, :, 128 * t:128 * t + 128] = (
                        part[:, b:b + 8].reshape(6, 64, 128).astype(BF16))
            return carry

        lax.fori_loop(0, K, slot, 0)

    pulls[0].wait()
    C0[0:K] = x_in[...].astype(F32).reshape(K, 4, 8, 8, 128)
    stage(0)
    entered()
    send_halo(0)

    for pull in pulls[1:]:
        pull.wait()
    for a in range(3):
        for t in range(9):
            WB[a, 128 * t:128 * t + 128, :] = conv_w[26 - 9 * a - t].astype(F32).T.astype(BF16)
    live = [jnp.where(nb[k, 13] >= 0, 1.0, 0.0).astype(F32) for k in range(K)]
    r_i = lax.broadcasted_iota(jnp.int32, (16, 64), 0)
    c_i = lax.broadcasted_iota(jnp.int32, (16, 64), 1)
    pool = ((r_i // 2 == c_i // 8) & (r_i % 2 == (c_i % 8) // 4)).astype(F32)
    r_j = lax.broadcasted_iota(jnp.int32, (64, 16), 1)
    c_j = lax.broadcasted_iota(jnp.int32, (64, 16), 0)
    unpool = ((r_j // 2 == c_j // 8) & (r_j % 2 == (c_j % 8) // 4)).astype(F32)
    cot_rows = jnp.concatenate(
        [cot_in[k].astype(F32).reshape(4, 2, 4, 8, 128).sum(axis=(0, 2)) * live[k]
         for k in range(K)], axis=0).reshape(64, 128)
    dz = jnp.dot(pool, cot_rows, precision=HIGH, preferred_element_type=F32).astype(BF16)
    grad_q = lax.dot_general(dz, up_w[...], (((1,), (1,)), ((), ())), preferred_element_type=F32)
    depth = jnp.concatenate([depth_w[...].astype(F32), jnp.zeros((5, 256), F32)], axis=0)
    turn_r = lax.broadcasted_iota(jnp.int32, (32, 32), 0)
    turn_c = lax.broadcasted_iota(jnp.int32, (32, 32), 1)
    turned = jnp.dot((turn_r + turn_c == 26).astype(F32), depth, precision=HIGH,
                     preferred_element_type=F32)

    def source(c, shape):
        t = lax.broadcasted_iota(jnp.int32, shape, 0)
        ys, xs = t // 3 % 3 + c // 2 + 1, t % 3 + c % 2 + 1
        block = 9 * (t // 9) + 3 * (ys // 2) + xs // 2
        base = (3 * (t // 9) + ys // 2) * 16 + ys % 2 * 2 + xs % 2
        return t, block, base

    found = []
    for c in range(4):
        t, block, _ = source(c, (32, 27))
        hit = ((block == lax.broadcasted_iota(jnp.int32, (32, 27), 1)) & (t < 27)).astype(F32)
        found.append(lax.dot_general(hit, nbv[...].astype(F32), (((1,), (1,)), ((), ())),
                                     precision=HIGH, preferred_element_type=F32))
    picks = []
    for k in range(K):
        for c in range(4):
            t, _, base = source(c, (32, 144))
            col = (lax.broadcasted_iota(jnp.int32, (32, 144), 1) - base).astype(F32)
            slot_of = found[c][:, k:k + 1]
            picks.append(((col == 4.0 * slot_of) & (slot_of >= 0.0) & (t < 27)).astype(F32))
    pick = jnp.concatenate(picks, axis=0).astype(BF16)
    WF[:, 9] = jnp.zeros((3, 128, 128), F32)

    wait_halo(0)
    build()
    for a in range(3):
        term = jnp.dot(T[a:a + 4].reshape(1024, 1152), conv_w[9 * a:9 * a + 9].reshape(1152, 128),
                       preferred_element_type=F32).reshape(4, K, 64, 128)
        if a == 0:
            FS[...] = term
        else:
            FS[...] += term
    field = FS[...]
    act = field * jax.nn.sigmoid(field)
    act_rows = act.sum(axis=0).reshape(K, 2, 4, 8, 128).sum(axis=2).reshape(64, 128)
    p = jnp.dot(pool, act_rows * (1.0 / 64.0), precision=HIGH, preferred_element_type=F32)
    p = p.astype(BF16)
    g = jnp.dot(p, down_w[...], preferred_element_type=F32).astype(BF16)
    GA[0, 4] = g
    send_coarse(0)
    wait_coarse(0)
    near = jnp.dot(pick, GA[0].reshape(144, 256), preferred_element_type=F32).reshape(16, 32, 256)
    v = g.astype(F32) + jnp.sum(near * depth[None], axis=1)
    dv = (grad_q * silu_slope(v)).astype(BF16)
    GA[1, 4] = dv
    send_coarse(1)
    dvf = dv.astype(F32)
    q = (v * jax.nn.sigmoid(v)).astype(BF16)
    up_part = lax.dot_general(q, dz, (((0,), (0,)), ((), ())), preferred_element_type=F32)
    lines = near[0] * dvf[0:1]
    for c in range(1, 16):
        lines = lines + near[c] * dvf[c:c + 1]
    DG[0:32] = lines[:, :128]
    DG[32:64] = lines[:, 128:]
    wait_coarse(1)
    near = jnp.dot(pick, GA[1].reshape(144, 256), preferred_element_type=F32).reshape(16, 32, 256)
    dg = (jnp.sum(near * turned[None], axis=1) + dvf).astype(BF16)
    dp = lax.dot_general(dg, down_w[...], (((1,), (1,)), ((), ())), preferred_element_type=F32)
    wide = jnp.dot(unpool, dp * (1.0 / 64.0), precision=HIGH, preferred_element_type=F32)
    wide = wide.reshape(K, 2, 8, 128)
    for k in range(K):
        up_rows = cot_in[k].astype(F32).reshape(4, 2, 4, 8, 128) + wide[k].reshape(1, 2, 1, 8, 128)
        slope = silu_slope(FS[:, k]).reshape(4, 2, 4, 8, 128)
        df = (up_rows * slope * live[k]).astype(BF16)
        DF[:, k] = df.reshape(4, 64, 128)
        C0[k] = df.astype(F32).reshape(4, 8, 8, 128)
    stage(1)
    send_halo(1)
    down_part = lax.dot_general(p, dg, (((0,), (0,)), ((), ())), preferred_element_type=F32)

    st1, rv1 = (st10, st11, st12), (rv10, rv11, rv12)
    st2, rv2 = (st20, st21, st22), (rv20, rv21, rv22)
    st3, rv3 = (st30, st31, st32), (rv30, rv31, rv32)
    Q = B * S
    mine = blk * S + slab

    def each(count, fn):
        def body(r, carry):
            fn(r)
            return carry
        lax.fori_loop(1, count, body, 0)

    def at_chip(q):
        return {"blk": lax.div(q, S), "slab": lax.rem(q, S), "ch": ch}

    def across(a):
        return copy(st1[a], rv1[a], p1s.at[a], p1r.at[a],
                    {"blk": blk, "slab": slab, "ch": 1 - ch})

    def along_slab(a):
        return copy(st2[a].at[1 - slab], rv2[a], p2s.at[a], p2r.at[a],
                    {"blk": blk, "slab": 1 - slab, "ch": ch})

    def along_blk(a, r):
        to = lax.rem(blk + r, B)
        return copy(st3[a].at[to], rv3[a].at[blk], p3s.at[a, r], p3r.at[a, r],
                    {"blk": to, "slab": slab, "ch": ch})

    def from_blk(a, r):
        src = lax.rem(blk - r + B, B)
        return copy(st3[a].at[src], rv3[a].at[src], p3s.at[a, r], p3r.at[a, r],
                    {"blk": src, "slab": slab, "ch": ch})

    def gather_out(r):
        to = lax.rem(mine + r, Q)
        return copy(ag.at[ch, mine], ag.at[ch, mine], gs.at[r], gr.at[r], at_chip(to))

    def gather_in(r):
        src = lax.rem(mine - r + Q, Q)
        return copy(ag.at[ch, src], ag.at[ch, src], gs.at[r], gr.at[r], at_chip(src))

    def gather_pair(side):
        return copy(ag.at[side], ag.at[side], gs.at[0], gr.at[0],
                    {"blk": blk, "slab": slab, "ch": 1 - ch})

    def step_core(a):
        for sl in range(S):
            for bk in range(B):
                at = pl.multiple_of(8 * ((bk * S + sl) * 2 + 1 - ch), 8)
                st1[a][sl, bk, 0:80] = WF[a, :, pl.ds(at, 8)].reshape(80, 128).astype(BF16)
        across(a).start()

    def step_slab(a):
        across(a).wait()
        for sl in range(S):
            for bk in range(B):
                at = pl.multiple_of(8 * ((bk * S + sl) * 2 + ch), 8)
                st2[a][sl, bk, 0:80] = (WF[a, :, pl.ds(at, 8)].reshape(80, 128)
                                        + rv1[a][sl, bk, 0:80].astype(F32)).astype(BF16)
                if a == 0:
                    st2[a][sl, bk, 80:128] = (SMALL[2 * (bk * S + sl) + ch]
                                              + rv1[a][sl, bk, 80:128].astype(F32)).astype(BF16)
        along_slab(a).start()

    def step_blk(a):
        along_slab(a).wait()
        st3[a][...] = (st2[a][slab].astype(F32) + rv2[a][...].astype(F32)).astype(BF16)
        each(B, lambda r: along_blk(a, r).start())

    def step_sum(a):
        each(B, lambda r: from_blk(a, r).wait())
        rv3[a][blk] = st3[a][blk]
        total = rv3[a][0].astype(F32)
        for bk in range(1, B):
            total = total + rv3[a][bk].astype(F32)
        cube = total[0:80].reshape(10, 8, 128)
        for i in range(8):
            cw_out[9 * a:9 * a + 9, 128 * i:128 * i + 128] = cube[0:9, i]
        return total

    if reduce:
        SMALL[:, 0:16] = up_part.reshape(16, 16, 128)
        SMALL[0:8, 16:32] = down_part[:, :128].reshape(8, 16, 128)
        SMALL[8:16, 16:32] = down_part[:, 128:].reshape(8, 16, 128)
        SMALL[0:4, 32:48] = DG[...].reshape(4, 16, 128)
        SMALL[4:16, 32:48] = jnp.zeros((12, 16, 128), F32)
        for sl in range(S):
            for bk in range(B):
                st10[sl, bk, 80:128] = SMALL[2 * (bk * S + sl) + 1 - ch].astype(BF16)
    else:
        up_out[...] = up_part
        dn_out[...] = down_part
        dp_out[:, :128] = DG[0:27]
        dp_out[:, 128:] = DG[32:59]

    for a in range(3):
        wg = lax.dot_general(T[a:a + 4].reshape(1024, 1152), DF[...].reshape(1024, 128),
                             (((0,), (0,)), ((), ())), preferred_element_type=F32)
        if reduce:
            WF[a, 0:9] = wg.reshape(9, 128, 128)
            step_core(a)
            if a > 0:
                step_slab(a - 1)
            if a > 1:
                step_blk(a - 2)
        else:
            cw_out[9 * a:9 * a + 9] = wg.reshape(9, 128, 128)
    if reduce:
        step_slab(2)
        step_blk(1)

    wait_halo(1)
    build()
    if reduce:
        step_blk(2)
        ag[ch, mine] = step_sum(0)[80:128].astype(BF16)
        each(Q, lambda r: gather_out(r).start())
    for a in range(3):
        term = jnp.dot(T[a:a + 4].reshape(1024, 1152), WB[a],
                       preferred_element_type=F32).reshape(4, K, 64, 128)
        if a == 0:
            FS[...] = term
        else:
            FS[...] += term
    for k in range(K):
        dx_out[k] = FS[:, k].reshape(256, 128).astype(BF16)
    pushes[0].start()

    if reduce:
        step_sum(1)
        each(Q, lambda r: gather_in(r).wait())
        gather_pair(ch).start()
        step_sum(2)
        pushes[1].start()
        gather_pair(1 - ch).wait()
        for c in range(2):
            for qi in range(8):
                d = 2 * qi + c
                up_out[16 * d:16 * d + 16] = ag[c, qi, 0:16].astype(F32)
                at, side = 16 * (d % 8), 128 * (d // 8)
                dn_out[at:at + 16, side:side + 128] = ag[c, qi, 16:32].astype(F32)
                if d < 4:
                    DG[16 * d:16 * d + 16] = ag[c, qi, 32:48].astype(F32)
        dp_out[:, :128] = DG[0:27]
        dp_out[:, 128:] = DG[32:59]
    for i, push in enumerate(pushes):
        if i > 1 or (i == 1 and not reduce):
            push.start()
    for push in pushes:
        push.wait()


def write_kernel(*refs):
    ins, outs, held, sem_in, sem_out = refs[0:5], refs[5:10], refs[10:15], refs[15], refs[16]
    reads = [pltpu.make_async_copy(ins[i], held[i], sem_in.at[i]) for i in range(5)]
    writes = [pltpu.make_async_copy(held[i], outs[i], sem_out.at[i]) for i in range(5)]
    for read in reads:
        read.start()
    for read, write in zip(reads, writes):
        read.wait()
        write.start()
    for write in writes:
        write.wait()


def per_device(
    mesh_sizes, fine_input, cotangent, conv_weight, down_weight, depth_weight, up_weight, slot_x, neighbours
):
    B, S, H = mesh_sizes
    n = B * S * H
    reduce = (B, S, H) == (4, 2, 2)
    nb = neighbours[0, 0]
    hbm = pl.BlockSpec(memory_space=pltpu.HBM)
    dma = pltpu.SemaphoreType.DMA
    V = pltpu.VMEM
    taps = (27, 1024) if reduce else (27, 128, 128)
    part_rows = (128, 80, 80)
    outs = pl.pallas_call(
        functools.partial(level_kernel, mesh_sizes, reduce),
        out_shape=(
            jax.ShapeDtypeStruct((4, 256, 128), BF16),
            jax.ShapeDtypeStruct(taps, F32),
            jax.ShapeDtypeStruct((128, 256), F32),
            jax.ShapeDtypeStruct((27, 256), F32),
            jax.ShapeDtypeStruct((256, 128), F32),
        ),
        in_specs=[hbm] * 7,
        out_specs=(hbm,) * 5,
        scratch_shapes=[
            V((5, 4, 8, 8, 128), F32), V((2, 5, 8, 8, 128), F32), V((2, 5, 4, 8, 128), F32),
            V((4, 5, 8, 128), F32),
            V((2, 2, 256, 128), BF16), V((2, 2, 128, 128), BF16), V((2, 4, 32, 128), BF16),
            V((2, 2, 256, 128), BF16), V((2, 2, 128, 128), BF16), V((2, 4, 32, 128), BF16),
            V((3, 6, 10, 8, 128), F32), V((6, 4, 64, 1152), BF16), V((4, 4, 64, 128), F32),
            V((4, 4, 64, 128), BF16), V((3, 1152, 128), BF16), V((2, 9, 16, 256), BF16),
            V((3, 10, 128, 128), F32),
            *[V((2, B, rows, 128), BF16) for rows in part_rows],
            *[V((2, B, rows, 128), BF16) for rows in part_rows],
            *[V((2, B, rows, 128), BF16) for rows in part_rows],
            *[V((B, rows, 128), BF16) for rows in part_rows],
            *[V((B, rows, 128), BF16) for rows in part_rows],
            *[V((B, rows, 128), BF16) for rows in part_rows],
            V((2, 8, 48, 128), BF16),
            V((64, 128), F32), V((16, 48, 128), F32),
            V((4, 256, 128), BF16), V((4, 256, 128), BF16), V((27, 128, 128), BF16),
            V((128, 256), BF16), V((256, 128), BF16),
            pltpu.SMEM((4, 27), jnp.int32), V((4, 27), jnp.int32), V((27, 256), BF16),
            V((4, 256, 128), BF16), V(taps, F32), V((128, 256), F32), V((27, 256), F32),
            V((256, 128), F32),
            dma((2, 8)), dma((2, 8)), dma((2, 8)), dma((2, 8)),
            dma((3,)), dma((3,)), dma((3,)), dma((3,)), dma((3, 4)), dma((3, 4)),
            dma((8,)), dma((8,)), dma((8,)), dma((5,)),
        ],
        compiler_params=pltpu.CompilerParams(
            collective_id=0, has_side_effects=True, vmem_limit_bytes=GRANT),
        name="level_pair",
    )(nb, depth_weight, fine_input[0, 0], cotangent[0, 0], conv_weight, down_weight, up_weight)
    dx, cw, dn, dp, up = outs
    if reduce:
        dx, cw, dn, dp, up = pl.pallas_call(
            write_kernel,
            out_shape=(dx, cw, dn, dp, up),
            in_specs=[hbm] * 5,
            out_specs=(hbm,) * 5,
            scratch_shapes=[V((4, 256, 128), BF16), V(taps, F32), V((128, 256), F32),
                            V((27, 256), F32), V((256, 128), F32), dma((5,)), dma((5,))],
            compiler_params=pltpu.CompilerParams(vmem_limit_bytes=GRANT),
            name="write_out",
        )(dx, cw, dn, dp, up)
    else:
        axes = ("blk", "slab", "ch")
        dn, dp, up = lax.psum((dn, dp, up), axes)
        cw = lax.psum_scatter(cw.reshape(27, 128 * 128), axes, scatter_dimension=1, tiled=True)
    return dx.reshape(fine_input.shape), cw, dn, dp, up


def solution(mesh):
    sizes = (mesh.shape["blk"], mesh.shape["slab"], mesh.shape["ch"])
    fine = P(("groups", "slab", "ch"), "blk", None, None, None)
    in_specs = (
        fine, fine, P(), P(), P(), P(),
        P(("groups", "slab", "ch"), "blk", None),
        P(("groups", "slab", "ch"), "blk", None, None),
    )
    out_specs = (
        fine,
        P("groups", ("blk", "slab", "ch")),
        P("groups", None),
        P("groups", None),
        P("groups", None),
    )
    return jax.shard_map(
        functools.partial(per_device, sizes), mesh=mesh, in_specs=in_specs, out_specs=out_specs,
        check_vma=False)
```

```python
import functools

import jax
import jax.numpy as jnp
from jax import lax
from jax.experimental import pallas as pl
from jax.experimental.pallas import tpu as pltpu
from jax.sharding import PartitionSpec as P

F32 = jnp.float32
BF16 = jnp.bfloat16
GRANT = 64 * 1024 * 1024 - 128 * 1024
HIGH = lax.Precision.HIGHEST
DIRS = [(da, db) for da in (-1, 0, 1) for db in (-1, 0, 1) if (da, db) != (0, 0)]


def silu_slope(value):
    sigma = jax.nn.sigmoid(value)
    return sigma * (1.0 + value * (1.0 - sigma))


def level_kernel(
    sizes, reduce, nb_hbm, depth_hbm, x_hbm, cot_hbm, conv_hbm, down_hbm, up_hbm,
    dx_hbm, cw_hbm, dn_hbm, dp_hbm, up_out_hbm,
    C0, NZ, NY, NC, hz, hy, hc, sz, sy, sc, FR, T, FS, DW, WB, GA, WF,
    st10, st11, st12, rv10, rv11, rv12, st20, st21, st22, rv20, rv21, rv22,
    st30, st31, st32, rv30, rv31, rv32, ag, DG, SMALL, x_in, cot_in, conv_w, down_w, up_w,
    nb, nbv, depth_w, dx_out, cw_out, dn_out, dp_out, up_out,
    hs, hr, cs, cr, p1s, p1r, p2s, p2r, p3s, p3r, gs, gr, ls, os,
):
    B, S, H = sizes
    K = 4
    blk, slab, ch = lax.axis_index("blk"), lax.axis_index("slab"), lax.axis_index("ch")
    row = slab * H + ch
    rows = S * H
    n = B * S * H
    me = blk * rows + row

    def target(d):
        return {"blk": lax.div(d, rows), "slab": lax.rem(lax.div(d, H), S), "ch": lax.rem(d, H)}

    def exists(da, db):
        r, c = row + da, blk + db
        return (r >= 0) & (r < rows) & (c >= 0) & (c < B)

    def beside(da, db):
        return target((blk + db) * rows + row + da)

    pulls = [pltpu.make_async_copy(src, dst, ls.at[i]) for i, (src, dst) in enumerate((
        (x_hbm, x_in), (cot_hbm, cot_in), (nb_hbm, nb), (nb_hbm, nbv), (depth_hbm, depth_w),
        (up_hbm, up_w), (down_hbm, down_w), (conv_hbm, conv_w)))]
    pushes = [pltpu.make_async_copy(src, dst, os.at[i]) for i, (src, dst) in enumerate((
        (dx_out, dx_hbm), (cw_out, cw_hbm), (dn_out, dn_hbm), (dp_out, dp_hbm), (up_out, up_out_hbm)))]
    for pull in pulls:
        pull.start()

    for ref in (hz, hy, hc, GA):
        ref[...] = jnp.zeros(ref.shape, ref.dtype)
    C0[K] = jnp.zeros(C0.shape[1:], F32)
    NZ[:, K] = jnp.zeros((2,) + NZ.shape[2:], F32)
    NY[:, K] = jnp.zeros((2,) + NY.shape[2:], F32)
    NC[:, K] = jnp.zeros((4,) + NC.shape[2:], F32)
    barrier = pltpu.get_barrier_semaphore()
    if reduce:
        def greet(r, carry):
            pl.semaphore_signal(barrier, inc=1, device_id=target(lax.rem(me + r, n)),
                                device_id_type=pl.DeviceIdType.MESH)
            return carry
        lax.fori_loop(1, n, greet, 0)
    else:
        for da, db in DIRS:
            @pl.when(exists(da, db))
            def _():
                pl.semaphore_signal(barrier, inc=1, device_id=beside(da, db),
                                    device_id_type=pl.DeviceIdType.MESH)

    def entered():
        if reduce:
            pl.semaphore_wait(barrier, n - 1)
        else:
            for da, db in DIRS:
                @pl.when(exists(da, db))
                def _():
                    pl.semaphore_wait(barrier, 1)

    def copy(src, dst, s, r, dev):
        return pltpu.make_async_remote_copy(
            src_ref=src, dst_ref=dst, send_sem=s, recv_sem=r, device_id=dev,
            device_id_type=pl.DeviceIdType.MESH)

    def face(ph, i, send):
        da, db = DIRS[i]
        if db == 0:
            return (sz if send else hz).at[ph, int(da > 0)]
        if da == 0:
            return (sy if send else hy).at[ph, int(db > 0)]
        return (sc if send else hc).at[ph, 2 * int(da > 0) + int(db > 0)]

    def stage(ph):
        for s in (0, 1):
            sz[ph, s] = C0[0:K, 3 * s].reshape(K * 64, 128).astype(BF16)
            sy[ph, s] = C0[0:K, :, 7 * s].reshape(K * 32, 128).astype(BF16)
            for u in (0, 1):
                sc[ph, 2 * s + u] = C0[0:K, 3 * s, 7 * u].reshape(K * 8, 128).astype(BF16)

    def send_halo(ph):
        for i, (da, db) in enumerate(DIRS):
            @pl.when(exists(da, db))
            def _():
                copy(face(ph, i, True), face(ph, 7 - i, False), hs.at[ph, i], hr.at[ph, 7 - i],
                     beside(da, db)).start()

    def wait_halo(ph):
        for i, (da, db) in enumerate(DIRS):
            @pl.when(exists(da, db))
            def _():
                copy(face(ph, i, True), face(ph, i, False), hs.at[ph, i], hr.at[ph, i],
                     beside(da, db)).wait()
        NZ[:, 0:K] = hz[ph].astype(F32).reshape(2, K, 8, 8, 128)
        NY[:, 0:K] = hy[ph].astype(F32).reshape(2, K, 4, 8, 128)
        NC[:, 0:K] = hc[ph].astype(F32).reshape(4, K, 8, 128)

    def send_coarse(ph):
        for i, (da, db) in enumerate(DIRS):
            @pl.when(exists(da, db))
            def _():
                copy(GA.at[ph, 4], GA.at[ph, 4 - 3 * da - db], cs.at[ph, i], cr.at[ph, 7 - i],
                     beside(da, db)).start()

    def wait_coarse(ph):
        for i, (da, db) in enumerate(DIRS):
            @pl.when(exists(da, db))
            def _():
                copy(GA.at[ph, 4], GA.at[ph, 4 + 3 * da + db], cs.at[ph, i], cr.at[ph, i],
                     beside(da, db)).wait()

    def build():
        xi = lax.broadcasted_iota(jnp.int32, (60, 8, 128), 1)

        def slot(k, carry):
            for e in range(3):
                def at(a, b):
                    v = nb[k, 9 * a + 3 * b + e]
                    return jnp.where(v < 0, K, v)
                FR[e, 1:5, 1:9] = C0[at(1, 1)]
                FR[e, 1:5, 0] = NY[0, at(1, 0)]
                FR[e, 1:5, 9] = NY[1, at(1, 2)]
                FR[e, 0, 1:9] = NZ[0, at(0, 1)]
                FR[e, 5, 1:9] = NZ[1, at(2, 1)]
                FR[e, 0, 0] = NC[0, at(0, 0)]
                FR[e, 0, 9] = NC[1, at(0, 2)]
                FR[e, 5, 0] = NC[2, at(2, 0)]
                FR[e, 5, 9] = NC[3, at(2, 2)]
            mid = FR[1].reshape(60, 8, 128)
            first = pltpu.roll(jnp.where(xi == 7, FR[0].reshape(60, 8, 128), mid), 1, 1)
            last = pltpu.roll(jnp.where(xi == 0, FR[2].reshape(60, 8, 128), mid), 7, 1)
            for e, part in enumerate((first, mid, last)):
                part = part.reshape(6, 10, 8, 128)
                for b in range(3):
                    t = 3 * b + e
                    T[:, k, :, 128 * t:128 * t + 128] = (
                        part[:, b:b + 8].reshape(6, 64, 128).astype(BF16))
            return carry

        lax.fori_loop(0, K, slot, 0)

    pulls[0].wait()
    C0[0:K] = x_in[...].astype(F32).reshape(K, 4, 8, 8, 128)
    stage(0)
    entered()
    send_halo(0)

    for pull in pulls[1:]:
        pull.wait()
    for a in range(3):
        for t in range(9):
            WB[a, 128 * t:128 * t + 128, :] = conv_w[26 - 9 * a - t].astype(F32).T.astype(BF16)
    live = [jnp.where(nb[k, 13] >= 0, 1.0, 0.0).astype(F32) for k in range(K)]
    r_i = lax.broadcasted_iota(jnp.int32, (16, 64), 0)
    c_i = lax.broadcasted_iota(jnp.int32, (16, 64), 1)
    pool = ((r_i // 2 == c_i // 8) & (r_i % 2 == (c_i % 8) // 4)).astype(F32)
    r_j = lax.broadcasted_iota(jnp.int32, (64, 16), 1)
    c_j = lax.broadcasted_iota(jnp.int32, (64, 16), 0)
    unpool = ((r_j // 2 == c_j // 8) & (r_j % 2 == (c_j % 8) // 4)).astype(F32)
    cot_rows = jnp.concatenate(
        [cot_in[k].astype(F32).reshape(4, 2, 4, 8, 128).sum(axis=(0, 2)) * live[k]
         for k in range(K)], axis=0).reshape(64, 128)
    dz = jnp.dot(pool, cot_rows, precision=HIGH, preferred_element_type=F32).astype(BF16)
    grad_q = lax.dot_general(dz, up_w[...], (((1,), (1,)), ((), ())), preferred_element_type=F32)
    depth = jnp.concatenate([depth_w[...].astype(F32), jnp.zeros((5, 256), F32)], axis=0)
    turn_r = lax.broadcasted_iota(jnp.int32, (32, 32), 0)
    turn_c = lax.broadcasted_iota(jnp.int32, (32, 32), 1)
    turned = jnp.dot((turn_r + turn_c == 26).astype(F32), depth, precision=HIGH,
                     preferred_element_type=F32)

    def source(c, shape):
        t = lax.broadcasted_iota(jnp.int32, shape, 0)
        ys, xs = t // 3 % 3 + c // 2 + 1, t % 3 + c % 2 + 1
        block = 9 * (t // 9) + 3 * (ys // 2) + xs // 2
        base = (3 * (t // 9) + ys // 2) * 16 + ys % 2 * 2 + xs % 2
        return t, block, base

    found = []
    for c in range(4):
        t, block, _ = source(c, (32, 27))
        hit = ((block == lax.broadcasted_iota(jnp.int32, (32, 27), 1)) & (t < 27)).astype(F32)
        found.append(lax.dot_general(hit, nbv[...].astype(F32), (((1,), (1,)), ((), ())),
                                     precision=HIGH, preferred_element_type=F32))
    picks = []
    for k in range(K):
        for c in range(4):
            t, _, base = source(c, (32, 144))
            col = (lax.broadcasted_iota(jnp.int32, (32, 144), 1) - base).astype(F32)
            slot_of = found[c][:, k:k + 1]
            picks.append(((col == 4.0 * slot_of) & (slot_of >= 0.0) & (t < 27)).astype(F32))
    pick = jnp.concatenate(picks, axis=0).astype(BF16)
    WF[:, 9] = jnp.zeros((3, 128, 128), F32)
    DW[...] = jnp.zeros(DW.shape, BF16)

    wait_halo(0)
    build()
    for a in range(3):
        term = jnp.dot(T[a:a + 4].reshape(1024, 1152), conv_w[9 * a:9 * a + 9].reshape(1152, 128),
                       preferred_element_type=F32).reshape(4, K, 64, 128)
        if a == 0:
            FS[...] = term
        else:
            FS[...] += term
    field = FS[...]
    act = field * jax.nn.sigmoid(field)
    act_rows = act.sum(axis=0).reshape(K, 2, 4, 8, 128).sum(axis=2).reshape(64, 128)
    p = jnp.dot(pool, act_rows * (1.0 / 64.0), precision=HIGH, preferred_element_type=F32)
    p = p.astype(BF16)
    g = jnp.dot(p, down_w[...], preferred_element_type=F32).astype(BF16)
    GA[0, 4] = g
    send_coarse(0)
    wait_coarse(0)
    near = jnp.dot(pick, GA[0].reshape(144, 256), preferred_element_type=F32).reshape(16, 32, 256)
    v = g.astype(F32) + jnp.sum(near * depth[None], axis=1)
    dv = (grad_q * silu_slope(v)).astype(BF16)
    GA[1, 4] = dv
    send_coarse(1)
    dvf = dv.astype(F32)
    q = (v * jax.nn.sigmoid(v)).astype(BF16)
    up_part = lax.dot_general(q, dz, (((0,), (0,)), ((), ())), preferred_element_type=F32)
    lines = near[0] * dvf[0:1]
    for c in range(1, 16):
        lines = lines + near[c] * dvf[c:c + 1]
    DG[0:32] = lines[:, :128]
    DG[32:64] = lines[:, 128:]
    wait_coarse(1)
    near = jnp.dot(pick, GA[1].reshape(144, 256), preferred_element_type=F32).reshape(16, 32, 256)
    dg = (jnp.sum(near * turned[None], axis=1) + dvf).astype(BF16)
    dp = lax.dot_general(dg, down_w[...], (((1,), (1,)), ((), ())), preferred_element_type=F32)
    wide = jnp.dot(unpool, dp * (1.0 / 64.0), precision=HIGH, preferred_element_type=F32)
    wide = wide.reshape(K, 2, 8, 128)
    for k in range(K):
        up_rows = cot_in[k].astype(F32).reshape(4, 2, 4, 8, 128) + wide[k].reshape(1, 2, 1, 8, 128)
        slope = silu_slope(FS[:, k]).reshape(4, 2, 4, 8, 128)
        df = (up_rows * slope * live[k]).astype(BF16)
        for u in range(3):
            DW[u:u + 4, k, :, 128 * u:128 * u + 128] = df.reshape(4, 64, 128)
        C0[k] = df.astype(F32).reshape(4, 8, 8, 128)
    stage(1)
    send_halo(1)
    down_part = lax.dot_general(p, dg, (((0,), (0,)), ((), ())), preferred_element_type=F32)

    st1, rv1 = (st10, st11, st12), (rv10, rv11, rv12)
    st2, rv2 = (st20, st21, st22), (rv20, rv21, rv22)
    st3, rv3 = (st30, st31, st32), (rv30, rv31, rv32)
    Q = B * S
    mine = blk * S + slab

    def each(count, fn):
        def body(r, carry):
            fn(r)
            return carry
        lax.fori_loop(1, count, body, 0)

    def at_chip(q):
        return {"blk": lax.div(q, S), "slab": lax.rem(q, S), "ch": ch}

    def across(a):
        return copy(st1[a], rv1[a], p1s.at[a], p1r.at[a],
                    {"blk": blk, "slab": slab, "ch": 1 - ch})

    def along_slab(a):
        return copy(st2[a].at[1 - slab], rv2[a], p2s.at[a], p2r.at[a],
                    {"blk": blk, "slab": 1 - slab, "ch": ch})

    def along_blk(a, r):
        to = lax.rem(blk + r, B)
        return copy(st3[a].at[to], rv3[a].at[blk], p3s.at[a, r], p3r.at[a, r],
                    {"blk": to, "slab": slab, "ch": ch})

    def from_blk(a, r):
        src = lax.rem(blk - r + B, B)
        return copy(st3[a].at[src], rv3[a].at[src], p3s.at[a, r], p3r.at[a, r],
                    {"blk": src, "slab": slab, "ch": ch})

    def gather_out(r):
        to = lax.rem(mine + r, Q)
        return copy(ag.at[ch, mine], ag.at[ch, mine], gs.at[r], gr.at[r], at_chip(to))

    def gather_in(r):
        src = lax.rem(mine - r + Q, Q)
        return copy(ag.at[ch, src], ag.at[ch, src], gs.at[r], gr.at[r], at_chip(src))

    def gather_pair(side):
        return copy(ag.at[side], ag.at[side], gs.at[0], gr.at[0],
                    {"blk": blk, "slab": slab, "ch": 1 - ch})

    def step_core(a):
        for sl in range(S):
            for bk in range(B):
                at = pl.multiple_of(8 * ((bk * S + sl) * 2 + 1 - ch), 8)
                st1[a][sl, bk, 0:80] = WF[a, :, pl.ds(at, 8)].reshape(80, 128).astype(BF16)
        across(a).start()

    def step_slab(a):
        across(a).wait()
        for sl in range(S):
            for bk in range(B):
                at = pl.multiple_of(8 * ((bk * S + sl) * 2 + ch), 8)
                st2[a][sl, bk, 0:80] = (WF[a, :, pl.ds(at, 8)].reshape(80, 128)
                                        + rv1[a][sl, bk, 0:80].astype(F32)).astype(BF16)
                if a == 0:
                    st2[a][sl, bk, 80:128] = (SMALL[2 * (bk * S + sl) + ch]
                                              + rv1[a][sl, bk, 80:128].astype(F32)).astype(BF16)
        along_slab(a).start()

    def step_blk(a):
        along_slab(a).wait()
        st3[a][...] = (st2[a][slab].astype(F32) + rv2[a][...].astype(F32)).astype(BF16)
        each(B, lambda r: along_blk(a, r).start())

    def step_sum(a):
        each(B, lambda r: from_blk(a, r).wait())
        rv3[a][blk] = st3[a][blk]
        total = rv3[a][0].astype(F32)
        for bk in range(1, B):
            total = total + rv3[a][bk].astype(F32)
        cube = total[0:80].reshape(10, 8, 128)
        for i in range(8):
            for u in range(3):
                cw_out[9 * u + 3 * a:9 * u + 3 * a + 3, 128 * i:128 * i + 128] = (
                    cube[3 * u:3 * u + 3, i])
        return total

    if reduce:
        SMALL[:, 0:16] = up_part.reshape(16, 16, 128)
        SMALL[0:8, 16:32] = down_part[:, :128].reshape(8, 16, 128)
        SMALL[8:16, 16:32] = down_part[:, 128:].reshape(8, 16, 128)
        SMALL[0:4, 32:48] = DG[...].reshape(4, 16, 128)
        SMALL[4:16, 32:48] = jnp.zeros((12, 16, 128), F32)
        for sl in range(S):
            for bk in range(B):
                st10[sl, bk, 80:128] = SMALL[2 * (bk * S + sl) + 1 - ch].astype(BF16)
    else:
        up_out[...] = up_part
        dn_out[...] = down_part
        dp_out[:, :128] = DG[0:27]
        dp_out[:, 128:] = DG[32:59]

    for a in range(3):
        wg = lax.dot_general(T[:, :, :, 384 * a:384 * a + 384].reshape(1536, 384),
                             DW[...].reshape(1536, 384),
                             (((0,), (0,)), ((), ())), preferred_element_type=F32)
        if reduce:
            for u in range(3):
                WF[a, 3 * u:3 * u + 3] = wg[:, 128 * u:128 * u + 128].reshape(3, 128, 128)
            step_core(a)
            if a > 0:
                step_slab(a - 1)
            if a > 1:
                step_blk(a - 2)
        else:
            for u in range(3):
                cw_out[9 * u + 3 * a:9 * u + 3 * a + 3] = (
                    wg[:, 128 * u:128 * u + 128].reshape(3, 128, 128))
    if reduce:
        step_slab(2)
        step_blk(1)

    wait_halo(1)
    build()
    if reduce:
        step_blk(2)
        ag[ch, mine] = step_sum(0)[80:128].astype(BF16)
        each(Q, lambda r: gather_out(r).start())
    for a in range(3):
        term = jnp.dot(T[a:a + 4].reshape(1024, 1152), WB[a],
                       preferred_element_type=F32).reshape(4, K, 64, 128)
        if a == 0:
            FS[...] = term
        else:
            FS[...] += term
    for k in range(K):
        dx_out[k] = FS[:, k].reshape(256, 128).astype(BF16)
    pushes[0].start()

    if reduce:
        step_sum(1)
        each(Q, lambda r: gather_in(r).wait())
        gather_pair(ch).start()
        step_sum(2)
        pushes[1].start()
        gather_pair(1 - ch).wait()
        for c in range(2):
            for qi in range(8):
                d = 2 * qi + c
                up_out[16 * d:16 * d + 16] = ag[c, qi, 0:16].astype(F32)
                at, side = 16 * (d % 8), 128 * (d // 8)
                dn_out[at:at + 16, side:side + 128] = ag[c, qi, 16:32].astype(F32)
                if d < 4:
                    DG[16 * d:16 * d + 16] = ag[c, qi, 32:48].astype(F32)
        dp_out[:, :128] = DG[0:27]
        dp_out[:, 128:] = DG[32:59]
    for i, push in enumerate(pushes):
        if i > 1 or (i == 1 and not reduce):
            push.start()
    for push in pushes:
        push.wait()


def write_kernel(*refs):
    ins, outs, held, sem_in, sem_out = refs[0:5], refs[5:10], refs[10:15], refs[15], refs[16]
    reads = [pltpu.make_async_copy(ins[i], held[i], sem_in.at[i]) for i in range(5)]
    writes = [pltpu.make_async_copy(held[i], outs[i], sem_out.at[i]) for i in range(5)]
    for read in reads:
        read.start()
    for read, write in zip(reads, writes):
        read.wait()
        write.start()
    for write in writes:
        write.wait()


def per_device(
    mesh_sizes, fine_input, cotangent, conv_weight, down_weight, depth_weight, up_weight, slot_x, neighbours
):
    B, S, H = mesh_sizes
    n = B * S * H
    reduce = (B, S, H) == (4, 2, 2)
    nb = neighbours[0, 0]
    hbm = pl.BlockSpec(memory_space=pltpu.HBM)
    dma = pltpu.SemaphoreType.DMA
    V = pltpu.VMEM
    taps = (27, 1024) if reduce else (27, 128, 128)
    part_rows = (128, 80, 80)
    outs = pl.pallas_call(
        functools.partial(level_kernel, mesh_sizes, reduce),
        out_shape=(
            jax.ShapeDtypeStruct((4, 256, 128), BF16),
            jax.ShapeDtypeStruct(taps, F32),
            jax.ShapeDtypeStruct((128, 256), F32),
            jax.ShapeDtypeStruct((27, 256), F32),
            jax.ShapeDtypeStruct((256, 128), F32),
        ),
        in_specs=[hbm] * 7,
        out_specs=(hbm,) * 5,
        scratch_shapes=[
            V((5, 4, 8, 8, 128), F32), V((2, 5, 8, 8, 128), F32), V((2, 5, 4, 8, 128), F32),
            V((4, 5, 8, 128), F32),
            V((2, 2, 256, 128), BF16), V((2, 2, 128, 128), BF16), V((2, 4, 32, 128), BF16),
            V((2, 2, 256, 128), BF16), V((2, 2, 128, 128), BF16), V((2, 4, 32, 128), BF16),
            V((3, 6, 10, 8, 128), F32), V((6, 4, 64, 1152), BF16), V((4, 4, 64, 128), F32),
            V((6, 4, 64, 384), BF16), V((3, 1152, 128), BF16), V((2, 9, 16, 256), BF16),
            V((3, 10, 128, 128), F32),
            *[V((2, B, rows, 128), BF16) for rows in part_rows],
            *[V((2, B, rows, 128), BF16) for rows in part_rows],
            *[V((2, B, rows, 128), BF16) for rows in part_rows],
            *[V((B, rows, 128), BF16) for rows in part_rows],
            *[V((B, rows, 128), BF16) for rows in part_rows],
            *[V((B, rows, 128), BF16) for rows in part_rows],
            V((2, 8, 48, 128), BF16),
            V((64, 128), F32), V((16, 48, 128), F32),
            V((4, 256, 128), BF16), V((4, 256, 128), BF16), V((27, 128, 128), BF16),
            V((128, 256), BF16), V((256, 128), BF16),
            pltpu.SMEM((4, 27), jnp.int32), V((4, 27), jnp.int32), V((27, 256), BF16),
            V((4, 256, 128), BF16), V(taps, F32), V((128, 256), F32), V((27, 256), F32),
            V((256, 128), F32),
            dma((2, 8)), dma((2, 8)), dma((2, 8)), dma((2, 8)),
            dma((3,)), dma((3,)), dma((3,)), dma((3,)), dma((3, 4)), dma((3, 4)),
            dma((8,)), dma((8,)), dma((8,)), dma((5,)),
        ],
        compiler_params=pltpu.CompilerParams(
            collective_id=0, has_side_effects=True, vmem_limit_bytes=GRANT),
        name="level_pair",
    )(nb, depth_weight, fine_input[0, 0], cotangent[0, 0], conv_weight, down_weight, up_weight)
    dx, cw, dn, dp, up = outs
    if reduce:
        dx, cw, dn, dp, up = pl.pallas_call(
            write_kernel,
            out_shape=(dx, cw, dn, dp, up),
            in_specs=[hbm] * 5,
            out_specs=(hbm,) * 5,
            scratch_shapes=[V((4, 256, 128), BF16), V(taps, F32), V((128, 256), F32),
                            V((27, 256), F32), V((256, 128), F32), dma((5,)), dma((5,))],
            compiler_params=pltpu.CompilerParams(vmem_limit_bytes=GRANT),
            name="write_out",
        )(dx, cw, dn, dp, up)
    else:
        axes = ("blk", "slab", "ch")
        dn, dp, up = lax.psum((dn, dp, up), axes)
        cw = lax.psum_scatter(cw.reshape(27, 128 * 128), axes, scatter_dimension=1, tiled=True)
    return dx.reshape(fine_input.shape), cw, dn, dp, up


def solution(mesh):
    sizes = (mesh.shape["blk"], mesh.shape["slab"], mesh.shape["ch"])
    fine = P(("groups", "slab", "ch"), "blk", None, None, None)
    in_specs = (
        fine, fine, P(), P(), P(), P(),
        P(("groups", "slab", "ch"), "blk", None),
        P(("groups", "slab", "ch"), "blk", None, None),
    )
    out_specs = (
        fine,
        P("groups", ("blk", "slab", "ch")),
        P("groups", None),
        P("groups", None),
        P("groups", None),
    )
    return jax.shard_map(
        functools.partial(per_device, sizes), mesh=mesh, in_specs=in_specs, out_specs=out_specs,
        check_vma=False)
```
